128 devices in a mesh: pool: 8 (over y, core), tp: 16 (over z, x).
Axes of the slice: x: 4, y: 4, z: 4, core: 2. Of those that a mesh axis runs over, the one named last changes fastest.
Arguments:
- hidden_in: bfloat16 [2176, 8192], P('pool'), may hold values from -6 to 6
- norm_gain: float32 [8192], replicated, may hold values from 0.1 to 1.9
- w_query: bfloat16 [8192, 4096], P(None, 'tp'), may hold values from -0.0625 to 0.0625
- w_keyval: bfloat16 [8192, 1024], P(None, 'tp'), may hold values from -0.25 to 0.25
- w_out: bfloat16 [4096, 8192], P('tp'), may hold values from -0.09375 to 0.09375
- kv_store: bfloat16 [2048, 4, 2, 128, 128], P(('pool', 'tp')), may hold values from -130 to 130
- page_slots: int32 [8, 128, 3], P(None, ('pool', 'tp')), may hold values from 0 to 15, as said below
- page_counts: int32 [8, 128], P('pool'), may hold values from 1 to 3, 256 in all within a row
Outputs:
- layer_out: bfloat16 [2176, 8192], P('pool', 'tp')
The draws below stay inside these ranges and needn't reach their ends.
Inputs may be any that keep to these rules, and one draw needn't show every extreme that they name: `page_slots`: the 3 slots of one request and holder are distinct pages. Only slots c < page_counts[r, s] are read. `page_counts`: each row sums to 256; every request has some holder with exactly 3 pages.
All inputs are finite; a program needn't handle non-finite values.
Results may differ from the reference program's by a relative error of at most 0.02.
The reference program's roundings to bfloat16 on the way count: a program that leaves them out, or rounds other values in their place, can miss the bound.
Values may be sent and summed in bfloat16 or wider, within the bound.
A program may use at most 192 MiB of HBM per device.

```python
import math
import jax
import jax.numpy as jnp
import numpy as np
from jax import lax

D = 8192
H = 32
KVH = 4
HD = 128
PAGE = 128
CAP = 3
TURN = 256
PG_DEV = 16
ROWS = 272
REQS = 8
PREFIX_PAGES = 256
TOTAL_PAGES = 2048
DEVICES = 128


def draw_kv_store(key, part):
    key = jax.random.fold_in(key, 11)
    draw_key = jax.random.fold_in(key, 0)
    full_shape = (TOTAL_PAGES, KVH, 2, PAGE, HD)
    spread = jnp.array([3.0, 1.0], jnp.float32).reshape(1, 1, 2, 1, 1)
    normal_part = jnp.clip(jax.random.normal(draw_key, full_shape, jnp.float32), -6.0, 6.0)
    return (normal_part * spread).astype(jnp.bfloat16)


def draw_page_slots(key, part):
    key = jax.random.fold_in(key, 23)
    score_key, holder_key = jax.random.split(key, 2)
    raw = jax.random.randint(score_key, (REQS, DEVICES, PG_DEV), 0, 1 << 20, dtype=jnp.int32)
    scores = raw * PG_DEV + jnp.arange(PG_DEV, dtype=jnp.int32)[None, None, :]
    order = jnp.argsort(scores, axis=-1, stable=True).astype(jnp.int32)
    chosen = order[:, :, :CAP]
    planted = jnp.concatenate([jnp.array([0, PG_DEV - 1], jnp.int32), jnp.arange(1, CAP - 1, dtype=jnp.int32)])
    holder = jax.random.randint(holder_key, (), 0, DEVICES, dtype=jnp.int32)
    is_planted = (jnp.arange(REQS, dtype=jnp.int32)[:, None] == 0) & (jnp.arange(DEVICES, dtype=jnp.int32)[None, :] == holder)
    return jnp.where(is_planted[:, :, None], planted[None, None, :], chosen).astype(jnp.int32)


def block_levels(key, extent, pieces, smallest, top_value):
    def one(axis_at, parts):
        steps = jax.random.uniform(jax.random.fold_in(jax.random.fold_in(key, 6), axis_at), (parts,), jnp.float32, smallest / len(pieces), top_value / len(pieces))
        return jnp.repeat(jnp.exp(steps), extent[axis_at] // parts).reshape((-1,) + (1,) * (len(extent) - axis_at - 1))

    factor_of = one(*pieces[0])
    for cut in pieces[1:]:
        factor_of = factor_of * one(*cut)
    return factor_of


def profile(count, total, most, lean):
    portions = [(1 << 20) // math.isqrt(grade ** lean) + 1 for grade in range(2, count + 1)]
    surplus, holding = total - most - (count - 1), [1] * (count - 1)
    while surplus > 0:
        free = [i for i in range(count - 1) if holding[i] < most]
        mass, left = sum([portions[i] for i in free]), surplus
        for i in free:
            extra = min(most - holding[i], max(1, left * portions[i] // mass), surplus)
            holding[i] = holding[i] + extra
            surplus = surplus - extra
    return np.array([most] + holding)


def uneven_parts(key, number_of, total, limit, lean):
    if number_of == 2:
        one = jax.random.randint(key, (), max(1, total - limit), min(limit, total - 1) + 1)
        return jnp.stack([one, total - one])
    lengths = jnp.asarray(profile(number_of, total, limit, lean), jnp.int32)
    couples = (number_of - 1) // 2
    source_of, sink = lengths[1:1 + 2 * couples:2], lengths[2:2 + 2 * couples:2]
    slack = jnp.minimum(source_of - 1, limit - sink)
    shifted = jax.random.randint(jax.random.fold_in(key, 1), (couples,), 0, 1 << 20) % (slack + 1)
    lengths = lengths.at[1:1 + 2 * couples:2].set(source_of - shifted).at[2:2 + 2 * couples:2].set(sink + shifted)
    return lengths[jax.random.permutation(jax.random.fold_in(key, 2), number_of)]


def normal_values(stream_key, shape, scale, bound, cuts=(), held_as=jnp.bfloat16):
    values = jax.random.normal(stream_key, shape, jnp.float32) * scale
    if len(cuts) > 0:
        values = block_levels(stream_key, shape, cuts, -0.22, 0.18) * values
    return jnp.clip(values, min=-bound, max=bound).astype(held_as)


def setup_inputs(seed: int = 0) -> dict:
    splits = jax.random.split(jax.random.key(seed), 9)
    hidden_in = normal_values(splits[0], (REQS * ROWS, D), 1.0, 6.0, ((0, 8),))
    norm_gain = jnp.clip(1.0 + 0.18 * jax.random.normal(splits[1], (D,), jnp.float32), 0.1, 1.9)
    w_query = normal_values(splits[2], (D, H * HD), D ** -0.5, 0.0625, ((1, 16),))
    w_keyval = normal_values(splits[3], (D, 2 * KVH * HD), (D // 16) ** -0.5, 0.25, ((1, 16),))
    w_out = normal_values(splits[4], (H * HD, D), (H * HD) ** -0.5, 0.09375, ((0, 16),))
    kv_store = draw_kv_store(jax.random.fold_in(splits[8], 71), 0)
    page_slots = draw_page_slots(jax.random.fold_in(splits[8], 71), 0)
    page_counts = jax.vmap(lambda own: uneven_parts(own, DEVICES, PREFIX_PAGES, CAP, 2))(jax.random.split(splits[7], REQS)).reshape((REQS, DEVICES)).astype(jnp.int32)
    return {"hidden_in": hidden_in, "norm_gain": norm_gain, "w_query": w_query, "w_keyval": w_keyval, "w_out": w_out, "kv_store": kv_store, "page_slots": page_slots, "page_counts": page_counts}


def rms_norm(hidden_in, norm_gain):
    as_float = hidden_in.astype(jnp.float32)
    inverse = lax.rsqrt(lax.optimization_barrier(jnp.mean(as_float * as_float, axis=-1, keepdims=True)) + 1e-05)
    return (as_float * inverse * norm_gain).astype(jnp.bfloat16)

def allowed_pairs(row_count, turn_len):
    query_idx = jnp.arange(row_count, dtype=jnp.int32)[:, None]
    key_idx = jnp.arange(row_count, dtype=jnp.int32)[None, :]
    return (key_idx <= query_idx) & ((key_idx < turn_len) | (key_idx == query_idx))

def reference(hidden_in, norm_gain, w_query, w_keyval, w_out, kv_store, page_slots, page_counts):
    normed = rms_norm(hidden_in, norm_gain)
    queries = jnp.dot(normed, w_query, preferred_element_type=jnp.float32).astype(jnp.bfloat16)
    turn_kv = jnp.dot(normed, w_keyval, preferred_element_type=jnp.float32).astype(jnp.bfloat16)
    group_size = H // KVH
    score_scale = 1.0 / HD ** 0.5
    allowed = allowed_pairs(ROWS, TURN)
    holders = page_counts.shape[1]

    def one_request(request):
        start_row = (request * ROWS).astype(jnp.int32)
        req_queries = lax.dynamic_slice_in_dim(queries, start_row, ROWS, 0).reshape(ROWS, H, HD)
        req_kv = lax.dynamic_slice_in_dim(turn_kv, start_row, ROWS, 0).reshape(ROWS, 2, KVH, HD)
        slots = lax.dynamic_index_in_dim(page_slots, request, 0, keepdims=False)
        counts = lax.dynamic_index_in_dim(page_counts, request, 0, keepdims=False)
        page_ids = (jnp.arange(holders, dtype=jnp.int32)[:, None] * PG_DEV + slots).reshape(-1)
        live_slots = jnp.arange(CAP, dtype=jnp.int32)[None, :] < counts[:, None]
        live_keys = jnp.repeat(live_slots.reshape(-1), PAGE)
        cached = kv_store[page_ids]

        def one_head(head_idx):
            kv_index = head_idx // group_size
            head_queries = lax.dynamic_index_in_dim(req_queries, head_idx, 1, keepdims=False)
            head_pages = lax.dynamic_index_in_dim(cached, kv_index, 1, keepdims=False)
            key_rows = head_pages[:, 0].reshape(-1, HD)
            value_rows = head_pages[:, 1].reshape(-1, HD)
            own_keys = lax.dynamic_index_in_dim(req_kv[:, 0], kv_index, 1, keepdims=False)
            own_values = lax.dynamic_index_in_dim(req_kv[:, 1], kv_index, 1, keepdims=False)
            prefix_scores = jnp.dot(head_queries, key_rows.T, preferred_element_type=jnp.float32) * score_scale
            prefix_scores = jnp.where(live_keys[None, :], prefix_scores, -jnp.inf)
            local_scores = jnp.dot(head_queries, own_keys.T, preferred_element_type=jnp.float32) * score_scale
            local_scores = jnp.where(allowed, local_scores, -jnp.inf)
            row_max = jnp.maximum(lax.optimization_barrier(jnp.max(prefix_scores, axis=1)), lax.optimization_barrier(jnp.max(local_scores, axis=1)))
            prefix_probs = jnp.exp(prefix_scores - row_max[:, None])
            local_probs = jnp.exp(local_scores - row_max[:, None])
            weight_sum = lax.optimization_barrier(jnp.sum(prefix_probs, axis=1)) + lax.optimization_barrier(jnp.sum(local_probs, axis=1))
            blended = jnp.dot(prefix_probs.astype(jnp.bfloat16), value_rows, preferred_element_type=jnp.float32)
            blended = blended + jnp.dot(local_probs.astype(jnp.bfloat16), own_values, preferred_element_type=jnp.float32)
            return (blended / weight_sum[:, None]).astype(jnp.bfloat16)
        per_head = lax.map(one_head, jnp.arange(H, dtype=jnp.int32))
        return per_head.transpose(1, 0, 2).reshape(ROWS, H * HD)
    attended = lax.map(one_request, jnp.arange(REQS, dtype=jnp.int32)).reshape(REQS * ROWS, H * HD)
    return jnp.dot(attended, w_out, preferred_element_type=jnp.float32).astype(jnp.bfloat16)
```

```python
import math

import jax
import jax.numpy as jnp
from jax import lax
from jax.experimental import pallas as pl
from jax.experimental.pallas import tpu as pltpu
from jax.sharding import PartitionSpec as P

SAMP = 16
MESH = pl.DeviceIdType.MESH
F32 = jnp.float32
BF16 = jnp.bfloat16
PAGE = 128
HD = 128
CAP = 3
LOG2E = 1.4426950408889634
DEAD = 1e30
ROWS = 272
GROUP = 8
QROWS = GROUP * ROWS
BLOCK = 640
QPAD = 4 * BLOCK
TILE = 256
TILES = 9
PARTNERS = 32
CHUNK = 4
NT = (((1,), (1,)), ((), ()))
NN = (((1,), (0,)), ((), ()))


def rms_norm(hidden_in, norm_gain):
    as_float = hidden_in.astype(F32)
    inverse = lax.rsqrt(jnp.mean(as_float * as_float, axis=-1, keepdims=True) + 1e-05)
    return (as_float * inverse * norm_gain).astype(BF16)


def attention_kernel(
    slots_ref, counts_ref, q_ref, turn_ref, kv_ref, out_ref,
    send, recv, qall, acc, stat_m, stat_l, vt, part_out, part_in, lse_out, lse_in,
    kv_ssem, kv_rsem, q_ssem, q_rsem, o_ssem, o_rsem, s_ssem, s_rsem, a_ssem, a_rsem,
):
    pool = lax.axis_index("pool")
    tp = lax.axis_index("tp")
    y, c = pool // 2, pool % 2
    z, x = tp // 4, tp % 4
    scale = LOG2E / math.sqrt(HD)

    def offset_device(i):
        dy, dc, dz = i // 8, (i // 4) % 2, i % 4
        return ((y + dy) % 4) * 2 + (c + dc) % 2, (z + dz) % 4

    def x_peer(d):
        return (pool, z * 4 + (x + d) % 4)

    barrier = pltpu.get_barrier_semaphore()

    def greet(i, carry):
        dest_pool, dest_z = offset_device(i)
        pl.semaphore_signal(barrier, inc=1, device_id=(dest_pool, dest_z * 4 + x), device_id_type=MESH)
        return carry

    lax.fori_loop(1, PARTNERS, greet, 0)
    for d in (1, 2, 3):
        pl.semaphore_signal(barrier, inc=1, device_id=x_peer(d), device_id_type=MESH)

    def fill(i, carry):
        dest_pool, dest_z = offset_device(i)
        for slot in range(CAP):
            page = slots_ref[dest_pool * CAP + slot]
            send[i, slot] = kv_ref[page, dest_z]
        return carry

    for slot in range(CAP):
        recv[0, slot] = kv_ref[slots_ref[pool * CAP + slot], z]
    qall[pl.ds(QROWS, QPAD - QROWS), :] = jnp.zeros((QPAD - QROWS, HD), BF16)
    own_rows = pl.ds(pl.multiple_of(x * 2 * ROWS, 16), 2 * ROWS)
    qall[own_rows, :] = q_ref[...]
    pl.semaphore_wait(barrier, PARTNERS - 1 + 3)

    def q_copy(d):
        return pltpu.make_async_remote_copy(
            src_ref=q_ref, dst_ref=qall.at[own_rows], send_sem=q_ssem.at[d], recv_sem=q_rsem.at[d],
            device_id=x_peer(d), device_id_type=MESH)

    def kv_copy(i):
        dest_pool, dest_z = offset_device(i)
        return pltpu.make_async_remote_copy(
            src_ref=send.at[i], dst_ref=recv.at[i], send_sem=kv_ssem.at[i], recv_sem=kv_rsem.at[i],
            device_id=(dest_pool, dest_z * 4 + x), device_id_type=MESH)

    for d in (1, 2, 3):
        q_copy(d).start()

    def fill_send(i, carry):
        fill(i, carry)
        kv_copy(i).start()
        return carry

    lax.fori_loop(1, PARTNERS, fill_send, 0)

    acc[...] = jnp.zeros_like(acc)
    stat_m[...] = jnp.full_like(stat_m, -DEAD)
    stat_l[...] = jnp.zeros_like(stat_l)
    for d in (1, 2, 3):
        q_copy(d).wait()

    def visit(g, carry):
        @pl.loop(0, CHUNK)
        def _(k):
            @pl.when(g * CHUNK + k > 0)
            def _():
                kv_copy(g * CHUNK + k).wait_recv()

        live = []
        for k in range(CHUNK):
            i = g * CHUNK + k
            dy, dc, dz = i // 8, (i // 4) % 2, i % 4
            holder = (((y + 4 - dy) % 4) * 2 + (c + dc) % 2) * 16 + ((z + 4 - dz) % 4) * 4 + x
            count = counts_ref[holder]
            for slot in range(CAP):
                live.append(count > slot)
        pages = recv[pl.ds(g * CHUNK, CHUNK)]
        keys = pages[:, :, :PAGE, :].reshape(CHUNK * CAP * PAGE, HD)
        vt[...] = pages[:, :, PAGE:, :].reshape(CHUNK * CAP * PAGE, HD).T

        @pl.loop(0, TILES)
        def _(t):
            cols = pl.ds(pl.multiple_of(t * TILE, TILE), TILE)
            scores = lax.dot_general(keys, qall[cols, :], NT, preferred_element_type=F32)
            old_m = stat_m[:, cols]
            new_m = old_m
            for n in range(CHUNK * CAP):
                top = jnp.max(scores[n * PAGE:(n + 1) * PAGE], axis=0, keepdims=True)
                new_m = jnp.maximum(new_m, jnp.where(live[n], top, -DEAD))
            shift = new_m * scale
            total = stat_l[:, cols] * jnp.exp2(old_m * scale - shift)
            weights = []
            for n in range(CHUNK * CAP):
                probs = jnp.exp2(scores[n * PAGE:(n + 1) * PAGE] * scale - jnp.where(live[n], shift, DEAD))
                total = total + jnp.sum(probs, axis=0, keepdims=True)
                weights.append(probs.astype(BF16))
            blended = lax.dot_general(vt[...], jnp.concatenate(weights, axis=0), NN, preferred_element_type=F32)
            acc[:, cols] = acc[:, cols] * jnp.exp2(old_m * scale - shift) + blended
            stat_m[:, cols] = new_m
            stat_l[:, cols] = total

        return carry

    lax.fori_loop(0, PARTNERS // CHUNK, visit, 0)

    block = pl.ds(pl.multiple_of(x * BLOCK, 128), BLOCK)
    own_q = qall[pl.ds(pl.multiple_of(x * BLOCK, 128), BLOCK), :]
    turn_scores = lax.dot_general(turn_ref[0], own_q, NT, preferred_element_type=F32)
    key_idx = lax.broadcasted_iota(jnp.int32, (ROWS, BLOCK), 0)
    row_idx = (lax.broadcasted_iota(jnp.int32, (ROWS, BLOCK), 1) + x * BLOCK) % ROWS
    allowed = (key_idx <= row_idx) & ((key_idx < ROWS - SAMP) | (key_idx == row_idx))
    turn_scores = jnp.where(allowed, turn_scores, -DEAD)
    turn_m = jnp.max(turn_scores, axis=0, keepdims=True)
    turn_p = jnp.exp2(turn_scores * scale - turn_m * scale)
    turn_l = jnp.sum(turn_p, axis=0, keepdims=True)
    turn_o = lax.dot_general(turn_ref[1].T, turn_p.astype(BF16), NN, preferred_element_type=F32)
    turn_lse = turn_m * scale + jnp.log2(turn_l)

    def o_copy(d):
        return pltpu.make_async_remote_copy(
            src_ref=part_out.at[d], dst_ref=part_in.at[d], send_sem=o_ssem.at[d], recv_sem=o_rsem.at[d],
            device_id=x_peer(d), device_id_type=MESH)

    def s_copy(d):
        return pltpu.make_async_remote_copy(
            src_ref=lse_out.at[d], dst_ref=lse_in.at[d], send_sem=s_ssem.at[d], recv_sem=s_rsem.at[d],
            device_id=x_peer(d), device_id_type=MESH)

    for d in (2, 1, 3):
        cols = pl.ds(pl.multiple_of(((x + d) % 4) * BLOCK, 128), BLOCK)
        total = jnp.maximum(stat_l[:, cols], 1e-30)
        part_out[d] = (acc[:, cols] / total).astype(BF16)
        lse_out[d] = jnp.broadcast_to(stat_m[:, cols] * scale + jnp.log2(total), (8, BLOCK))
        o_copy(d).start()
        s_copy(d).start()

    own_l = jnp.maximum(stat_l[:, block], 1e-30)
    own_lse = stat_m[:, block] * scale + jnp.log2(own_l)
    for d in (1, 2, 3):
        o_copy(d).wait()
        s_copy(d).wait()
    lses = [lse_in[d][:1] for d in (1, 2, 3)]
    top = jnp.maximum(own_lse, turn_lse)
    for lse in lses:
        top = jnp.maximum(top, lse)
    own_w = jnp.exp2(own_lse - top)
    turn_w = jnp.exp2(turn_lse - top)
    norm = own_w + turn_w
    merged = acc[:, block] * (own_w / own_l) + turn_o * (turn_w / turn_l)
    for d in (1, 2, 3):
        w = jnp.exp2(lses[d - 1] - top)
        norm = norm + w
        merged = merged + part_in[d].astype(F32) * w
    attended = (merged / norm).T.astype(BF16)

    part_rows = pl.ds(pl.multiple_of(x * BLOCK, 128), BLOCK)
    qall[part_rows, :] = attended

    def a_copy(d):
        return pltpu.make_async_remote_copy(
            src_ref=qall.at[part_rows], dst_ref=out_ref.at[part_rows], send_sem=a_ssem.at[d],
            recv_sem=a_rsem.at[d], device_id=x_peer(d), device_id_type=MESH)

    for d in (2, 1, 3):
        a_copy(d).start()
    out_ref[part_rows, :] = attended
    for d in (1, 2, 3):
        a_copy(d).wait()

    @pl.loop(1, PARTNERS)
    def _(i):
        kv_copy(i).wait_send()


def attend(slots, counts, q, turn, kv):
    vmem = pl.BlockSpec(memory_space=pltpu.VMEM)
    smem = pl.BlockSpec(memory_space=pltpu.SMEM)
    dma = pltpu.SemaphoreType.DMA
    return pl.pallas_call(
        attention_kernel,
        out_shape=jax.ShapeDtypeStruct((QPAD, HD), BF16),
        in_specs=[smem, smem, vmem, vmem, vmem],
        out_specs=vmem,
        scratch_shapes=[
            pltpu.VMEM((PARTNERS, CAP, 2 * PAGE, HD), BF16),
            pltpu.VMEM((PARTNERS, CAP, 2 * PAGE, HD), BF16),
            pltpu.VMEM((QPAD, HD), BF16),
            pltpu.VMEM((HD, QPAD), F32),
            pltpu.VMEM((1, QPAD), F32),
            pltpu.VMEM((1, QPAD), F32),
            pltpu.VMEM((HD, CHUNK * CAP * PAGE), BF16),
            pltpu.VMEM((4, HD, BLOCK), BF16),
            pltpu.VMEM((4, HD, BLOCK), BF16),
            pltpu.VMEM((4, 8, BLOCK), F32),
            pltpu.VMEM((4, 8, BLOCK), F32),
            dma((PARTNERS,)), dma((PARTNERS,)),
            dma((4,)), dma((4,)), dma((4,)), dma((4,)), dma((4,)), dma((4,)), dma((4,)), dma((4,)),
        ],
        compiler_params=pltpu.CompilerParams(
            collective_id=1, has_side_effects=True, vmem_limit_bytes=56 * 2**20),
        cost_estimate=pl.CostEstimate(flops=14 * 10**9, bytes_accessed=8 * 10**6, transcendentals=27 * 10**6),
        name="attend",
    )(slots, counts, q, turn, kv)


def local(hidden_in, norm_gain, w_query, w_keyval, w_out, kv_store, page_slots, page_counts):
    row_count = hidden_in.shape[0]
    tp_rank = lax.axis_index("tp")
    z, x = tp_rank // 4, tp_rank % 4
    normed = rms_norm(hidden_in, norm_gain)
    queries = jnp.dot(normed, w_query, preferred_element_type=F32).astype(BF16)
    kv_piece = jnp.dot(normed, w_keyval, preferred_element_type=F32).astype(BF16)
    turn_kv = lax.all_gather(kv_piece, "tp", axis=1, tiled=True).reshape(row_count, 2, 4, HD)
    turn = lax.dynamic_index_in_dim(turn_kv, z, 2, keepdims=False).transpose(1, 0, 2)
    q = queries.reshape(row_count, 2, HD).transpose(1, 0, 2).reshape(2 * row_count, HD)
    everything = attend(
        page_slots.reshape(-1), page_counts.reshape(-1), q, turn,
        kv_store.reshape(16, 4, 2 * PAGE, HD))
    attended = lax.dynamic_slice_in_dim(everything, x * 2 * ROWS, 2 * ROWS, 0)
    attended = attended.reshape(2, ROWS, HD).transpose(1, 0, 2).reshape(ROWS, 2 * HD)
    summed = lax.psum_scatter(
        lax.dot_general(
            w_out, attended, (((0,), (1,)), ((), ())), preferred_element_type=F32
        ).astype(BF16),
        "tp",
        scatter_dimension=0,
        tiled=True,
    ).astype(F32)
    return summed.T.astype(BF16)


def solution(mesh):
    return jax.shard_map(
        local,
        mesh=mesh,
        in_specs=(
            P("pool", None),
            P(),
            P(None, "tp"),
            P(None, "tp"),
            P("tp", None),
            P(("pool", "tp"), None, None, None, None),
            P(None, ("pool", "tp"), None),
            P("pool", None),
        ),
        out_specs=P("pool", "tp"),
        check_vma=False,
    )
```

```python
import math

import jax
import jax.numpy as jnp
from jax import lax
from jax.experimental import pallas as pl
from jax.experimental.pallas import tpu as pltpu
from jax.sharding import PartitionSpec as P

SAMP = 16
MESH = pl.DeviceIdType.MESH
F32 = jnp.float32
BF16 = jnp.bfloat16
PAGE = 128
HD = 128
CAP = 3
D = 8192
LOG2E = 1.4426950408889634
DEAD = 1e30
ROWS = 272
GROUP = 8
QROWS = GROUP * ROWS
BLOCK = 640
QPAD = 4 * BLOCK
TILE = 256
TILES = 9
UNROLL = 3
SOURCES = 8
CHUNK = 4
KEYS = CHUNK * CAP * PAGE
PART = 512
OUT = 512
NT = (((1,), (1,)), ((), ()))
NN = (((1,), (0,)), ((), ()))
FAR_FIRST = (2, 1, 3)


def plane_offset(i):
    dy = jnp.where(i < 2, 0, jnp.where(i < 6, 1 + 2 * (i % 2), 2))
    dc = jnp.where((i >= 2) & (i < 6), (i - 2) // 2, i % 2)
    return dy, dc


def stage_offset(k):
    return jnp.where(k < 2, k, 5 - k)


def layer_kernel(
    slots_ref, counts_ref, gain_ref, hidden_hbm, wq_hbm, wkv_hbm, wout_hbm, kv_hbm, out_ref,
    hidden, wq, wkv, wout, held0, held1, held2, held3, slots_in, slots_smem,
    ysend, yrecv, squares, q_acc, kv_acc, qown, qall, piece, pieces, turn,
    acc, stat_m, stat_l, vt, turn_o, turn_lse,
    part_out, part_in, lse_out, lse_in, att_out, att_all, sum_out, sum_in,
    load_sem, wout_load_sem, slot_sem, zk_s, zk_r, zs_s, zs_r, zp_s, zp_r, y_s, y_r,
    xq_s, xq_r, xt_s, xt_r, xw_s, xw_r, xo_s, xo_r, xl_s, xl_r, xa_s, xa_r, zo_s, zo_r,
):
    pool = lax.axis_index("pool")
    tp = lax.axis_index("tp")
    y, c = pool // 2, pool % 2
    z, x = tp // 4, tp % 4
    scale = LOG2E / math.sqrt(HD)
    held = (held0, held1, held2, held3)

    def x_peer(d):
        return (pool, z * 4 + (x + d) % 4)

    def z_peer(d):
        return (pool, ((z + d) % 4) * 4 + x)

    def plane_peer(i):
        dy, dc = plane_offset(i)
        return ((y + dy) % 4) * 2 + (c + dc) % 2

    def remote(src, dst, send_sem, recv_sem, device):
        return pltpu.make_async_remote_copy(
            src_ref=src, dst_ref=dst, send_sem=send_sem, recv_sem=recv_sem, device_id=device, device_id_type=MESH)

    barrier = pltpu.get_barrier_semaphore()
    for i in range(1, SOURCES):
        pl.semaphore_signal(barrier, inc=1, device_id=(plane_peer(i), tp), device_id_type=MESH)
    for d in (1, 2, 3):
        pl.semaphore_signal(barrier, inc=1, device_id=x_peer(d), device_id_type=MESH)
        pl.semaphore_signal(barrier, inc=1, device_id=z_peer(d), device_id_type=MESH)

    own_pages = pltpu.make_async_copy(kv_hbm.at[:, z], held0, load_sem.at[0])
    own_pages.start()
    loads = [
        pltpu.make_async_copy(hidden_hbm, hidden, load_sem.at[1]),
        pltpu.make_async_copy(wq_hbm, wq, load_sem.at[2]),
        pltpu.make_async_copy(wkv_hbm, wkv, load_sem.at[3]),
    ]
    for load in loads:
        load.start()
    own_slots = pltpu.make_async_copy(slots_ref, slots_smem.at[0], slot_sem.at[0])
    own_slots.start()
    pl.semaphore_wait(barrier, SOURCES - 1 + 6)

    def slot_copy(d):
        return remote(slots_ref, slots_in.at[d], zs_s.at[d], zs_r.at[d], z_peer(d))

    def page_copy(d):
        return remote(kv_hbm.at[:, (z + d) % 4], held[d], zk_s.at[d], zk_r.at[d], z_peer(d))

    for d in (1, 3, 2):
        slot_copy(d).start()
    for d in (1, 3):
        page_copy(d).start()

    def y_copy(k, i):
        return remote(
            ysend.at[k, i], yrecv.at[k, i], y_s.at[k * SOURCES + i], y_r.at[k * SOURCES + i], (plane_peer(i), tp))

    def pass_on(k, d):
        for slot in range(CAP):
            yrecv[k, 0, slot] = held[d][slots_smem[d, pool, slot]]

        @pl.loop(1, SOURCES)
        def _(n):
            i = jnp.where(n < SOURCES - 1, n + 1, 1)
            dest = plane_peer(i)
            for slot in range(CAP):
                ysend[k, i, slot] = held[d][slots_smem[d, dest, slot]]
            y_copy(k, i).start()

    own_slots.wait()
    own_pages.wait()
    pass_on(0, 0)

    for load in loads:
        load.wait()
    squares[...] = jnp.zeros_like(squares)

    @pl.loop(0, D // PART)
    def _(n):
        part = hidden[:, pl.ds(pl.multiple_of(n * PART, PART), PART)].astype(F32)
        part = part * part
        for m in range(PART // 128):
            squares[...] += part[:, m * 128:(m + 1) * 128]

    mean = jnp.sum(squares[...], axis=1, keepdims=True) * (1.0 / D)
    squares[...] = jnp.broadcast_to(lax.rsqrt(mean + 1e-05), squares.shape)
    q_acc[...] = jnp.zeros_like(q_acc)
    kv_acc[...] = jnp.zeros_like(kv_acc)

    @pl.loop(0, D // PART)
    def _(n):
        cols = pl.ds(pl.multiple_of(n * PART, PART), PART)
        inverse = squares[:, :1]
        normed = (hidden[:, cols].astype(F32) * inverse * gain_ref[:, cols]).astype(BF16)
        q_acc[...] += jnp.dot(normed, wq[cols, :], preferred_element_type=F32)
        kv_acc[...] += lax.dot_general(normed, wkv[:, cols], NT, preferred_element_type=F32)

    queries = q_acc[...].astype(BF16)
    qown[:ROWS, :] = queries[:, :HD]
    qown[ROWS:, :] = queries[:, HD:]
    own_rows = pl.ds(pl.multiple_of(x * 2 * ROWS, 16), 2 * ROWS)

    def q_copy(d):
        return remote(qown, qall.at[own_rows], xq_s.at[d], xq_r.at[d], x_peer(d))

    for d in FAR_FIRST:
        q_copy(d).start()
    qall[own_rows, :] = qown[...]
    qall[pl.ds(QROWS, QPAD - QROWS), :] = jnp.zeros((QPAD - QROWS, HD), BF16)

    half = kv_acc[...]
    blank = jnp.zeros_like(half)
    piece[...] = jnp.where(
        x % 2 == 0, jnp.concatenate([half, blank], axis=1), jnp.concatenate([blank, half], axis=1)).astype(BF16)

    def piece_copy(d):
        return remote(piece, pieces.at[z], zp_s.at[d], zp_r.at[d], z_peer(d))

    for d in (1, 2, 3):
        piece_copy(d).start()
    pieces[z] = piece[...]

    def wout_copy(d, n):
        columns = pl.ds(pl.multiple_of((n * 4 + (x + d) % 4) * OUT, OUT), OUT)
        rows = pl.ds(pl.multiple_of(x * 256, 256), 256)
        return remote(wout_hbm.at[:, columns], wout.at[n, rows], xw_s.at[d * 4 + n], xw_r.at[d * 4 + n], x_peer(d))

    def own_wout(n):
        columns = pl.ds(pl.multiple_of((n * 4 + x) * OUT, OUT), OUT)
        rows = pl.ds(pl.multiple_of(x * 256, 256), 256)
        return pltpu.make_async_copy(wout_hbm.at[:, columns], wout.at[n, rows], wout_load_sem.at[n])

    acc[...] = jnp.zeros_like(acc)
    stat_m[...] = jnp.full_like(stat_m, -DEAD)
    stat_l[...] = jnp.zeros_like(stat_l)
    for d in (1, 2, 3):
        q_copy(d).wait()

    def turn_copy(d, kind):
        return remote(
            pieces.at[kind * 2 + z // 2], turn.at[kind, x], xt_s.at[d * 2 + kind], xt_r.at[d * 2 + kind], x_peer(d))

    def arrived(d, k):
        page_copy(d).wait_recv()
        slot_copy(d).wait_recv()
        to_smem = pltpu.make_async_copy(slots_in.at[d], slots_smem.at[d], slot_sem.at[d])
        to_smem.start()
        to_smem.wait()
        pass_on(k, d)

    def visit(n, carry):
        k, first = n // 2, (n % 2) * CHUNK

        @pl.loop(0, CHUNK)
        def _(j):
            @pl.when(first + j > 0)
            def _():
                y_copy(k, first + j).wait_recv()

        live = []
        for j in range(CHUNK):
            dy, dc = plane_offset(first + j)
            holder = (((y + 4 - dy) % 4) * 2 + (c + dc) % 2) * 16 + ((z + 4 - stage_offset(k)) % 4) * 4 + x
            count = counts_ref[holder]
            for slot in range(CAP):
                live.append(count > slot)
        pages = yrecv[k, pl.ds(first, CHUNK)]
        keys = pages[:, :, :PAGE, :].reshape(KEYS, HD)
        vt[...] = pages[:, :, PAGE:, :].reshape(KEYS, HD).T

        @pl.loop(0, TILES // UNROLL)
        def _(t):
            cols = [pl.ds(pl.multiple_of((t * UNROLL + u) * TILE, TILE), TILE) for u in range(UNROLL)]
            all_scores = [
                lax.dot_general(keys, qall[cols[u], :], NT, preferred_element_type=F32) for u in range(UNROLL)]
            for u in range(UNROLL):
                scores = all_scores[u]
                old_m = stat_m[:, cols[u]]
                new_m = old_m
                for j in range(CHUNK * CAP):
                    top = jnp.max(scores[j * PAGE:(j + 1) * PAGE], axis=0, keepdims=True)
                    new_m = jnp.maximum(new_m, jnp.where(live[j], top, -DEAD))
                shift = new_m * scale
                shrink = jnp.exp2(old_m * scale - shift)
                total = stat_l[:, cols[u]] * shrink
                weights = []
                for j in range(CHUNK * CAP):
                    probs = jnp.exp2(scores[j * PAGE:(j + 1) * PAGE] * scale - jnp.where(live[j], shift, DEAD))
                    total = total + jnp.sum(probs, axis=0, keepdims=True)
                    weights.append(probs.astype(BF16))
                blended = lax.dot_general(vt[...], jnp.concatenate(weights, axis=0), NN, preferred_element_type=F32)
                acc[:, cols[u]] = acc[:, cols[u]] * shrink + blended
                stat_m[:, cols[u]] = new_m
                stat_l[:, cols[u]] = total

        @pl.when(n == 0)
        def _():
            arrived(1, 1)
            arrived(3, 2)
            page_copy(2).start()
            for d in (1, 2, 3):
                piece_copy(d).wait()
            for d in FAR_FIRST:
                for kind in range(2):
                    turn_copy(d, kind).start()
            for kind in range(2):
                turn[kind, x] = pieces[kind * 2 + z // 2]
            for d in FAR_FIRST:
                for m in range(4):
                    wout_copy(d, m).start()
            for m in range(4):
                own_wout(m).start()

        @pl.when(n == 3)
        def _():
            arrived(2, 3)

        return carry

    lax.fori_loop(0, 2 * 4, visit, 0)

    for d in (1, 2, 3):
        for kind in range(2):
            turn_copy(d, kind).wait()
    pair = (z % 2) * 2
    turn_k = turn[0, pair] + turn[0, pair + 1]
    turn_v = turn[1, pair] + turn[1, pair + 1]
    block = pl.ds(pl.multiple_of(x * BLOCK, 128), BLOCK)
    turn_scores = lax.dot_general(turn_k, qall[block, :], NT, preferred_element_type=F32)
    key_idx = lax.broadcasted_iota(jnp.int32, (ROWS, BLOCK), 0)
    row_idx = (lax.broadcasted_iota(jnp.int32, (ROWS, BLOCK), 1) + x * BLOCK) % ROWS
    allowed = (key_idx <= row_idx) & ((key_idx < ROWS - SAMP) | (key_idx == row_idx))
    turn_scores = jnp.where(allowed, turn_scores, -DEAD)
    turn_m = jnp.max(turn_scores, axis=0, keepdims=True)
    turn_p = jnp.exp2(turn_scores * scale - turn_m * scale)
    turn_l = jnp.sum(turn_p, axis=0, keepdims=True)
    turn_o[...] = lax.dot_general(turn_v.T, turn_p.astype(BF16), NN, preferred_element_type=F32) / turn_l
    turn_lse[...] = turn_m * scale + jnp.log2(turn_l)

    def o_copy(d):
        return remote(part_out.at[d], part_in.at[d], xo_s.at[d], xo_r.at[d], x_peer(d))

    def l_copy(d):
        return remote(lse_out.at[d], lse_in.at[d], xl_s.at[d], xl_r.at[d], x_peer(d))

    for d in FAR_FIRST:
        cols = pl.ds(pl.multiple_of(((x + d) % 4) * BLOCK, 128), BLOCK)
        total = jnp.maximum(stat_l[:, cols], 1e-30)
        part_out[d] = (acc[:, cols] / total).astype(BF16)
        lse_out[d] = jnp.broadcast_to(stat_m[:, cols] * scale + jnp.log2(total), (8, BLOCK))
        o_copy(d).start()
        l_copy(d).start()

    own_l = jnp.maximum(stat_l[:, block], 1e-30)
    own_lse = stat_m[:, block] * scale + jnp.log2(own_l)
    for d in (1, 2, 3):
        o_copy(d).wait()
        l_copy(d).wait()
    lses = [lse_in[d][:1] for d in (1, 2, 3)]
    top = jnp.maximum(own_lse, turn_lse[...])
    for lse in lses:
        top = jnp.maximum(top, lse)
    own_w = jnp.exp2(own_lse - top)
    turn_w = jnp.exp2(turn_lse[...] - top)
    norm = own_w + turn_w
    merged = acc[:, block] * (own_w / own_l) + turn_o[...] * turn_w
    for d in (1, 2, 3):
        w = jnp.exp2(lses[d - 1] - top)
        norm = norm + w
        merged = merged + part_in[d].astype(F32) * w
    att_out[...] = (merged / norm).T.astype(BF16)

    def a_copy(d):
        return remote(att_out, att_all.at[block], xa_s.at[d], xa_r.at[d], x_peer(d))

    for d in FAR_FIRST:
        a_copy(d).start()
    att_all[block, :] = att_out[...]
    for d in (1, 2, 3):
        for m in range(4):
            wout_copy(d, m).wait()
    for m in range(4):
        own_wout(m).wait()
    for d in (1, 2, 3):
        a_copy(d).wait()

    attended = jnp.concatenate([att_all[h * ROWS:(h + 1) * ROWS, :] for h in range(GROUP)], axis=1)

    def z_copy(d):
        return remote(sum_out.at[d], sum_in.at[d], zo_s.at[d], zo_r.at[d], z_peer(d))

    for d in FAR_FIRST:
        sum_out[d] = jnp.dot(attended, wout[(z + d) % 4], preferred_element_type=F32).astype(BF16)
        z_copy(d).start()
    result = jnp.dot(attended, wout[z], preferred_element_type=F32)
    for d in (1, 2, 3):
        z_copy(d).wait()
        result = result + sum_in[d].astype(F32)
    out_ref[...] = result.astype(BF16)

    for d in (1, 2, 3):
        page_copy(d).wait_send()
        slot_copy(d).wait_send()

    @pl.loop(0, 4)
    def _(k):
        @pl.loop(1, SOURCES)
        def _(i):
            y_copy(k, i).wait_send()


def local(hidden_in, norm_gain, w_query, w_keyval, w_out, kv_store, page_slots, page_counts):
    vmem = pl.BlockSpec(memory_space=pltpu.VMEM)
    smem = pl.BlockSpec(memory_space=pltpu.SMEM)
    anywhere = pl.BlockSpec(memory_space=pl.ANY)
    dma = pltpu.SemaphoreType.DMA
    slots = jnp.pad(page_slots[:, 0, :], ((0, 0), (0, 128 - CAP)))
    return pl.pallas_call(
        layer_kernel,
        out_shape=jax.ShapeDtypeStruct((ROWS, OUT), BF16),
        in_specs=[vmem, smem, vmem, anywhere, anywhere, anywhere, anywhere, anywhere],
        out_specs=vmem,
        scratch_shapes=[
            pltpu.VMEM((ROWS, D), BF16),
            pltpu.VMEM((D, 256), BF16),
            pltpu.VMEM((64, D), BF16),
            pltpu.VMEM((4, 1024, OUT), BF16),
            pltpu.VMEM((16, 2 * PAGE, HD), BF16),
            pltpu.VMEM((16, 2 * PAGE, HD), BF16),
            pltpu.VMEM((16, 2 * PAGE, HD), BF16),
            pltpu.VMEM((16, 2 * PAGE, HD), BF16),
            pltpu.VMEM((4, 8, 128), jnp.int32),
            pltpu.SMEM((4, 8, 128), jnp.int32),
            pltpu.VMEM((4, SOURCES, CAP, 2 * PAGE, HD), BF16),
            pltpu.VMEM((4, SOURCES, CAP, 2 * PAGE, HD), BF16),
            pltpu.VMEM((ROWS, 128), F32),
            pltpu.VMEM((ROWS, 256), F32),
            pltpu.VMEM((ROWS, 64), F32),
            pltpu.VMEM((2 * ROWS, HD), BF16),
            pltpu.VMEM((QPAD, HD), BF16),
            pltpu.VMEM((ROWS, HD), BF16),
            pltpu.VMEM((4, ROWS, HD), BF16),
            pltpu.VMEM((2, 4, ROWS, HD), BF16),
            pltpu.VMEM((HD, QPAD), F32),
            pltpu.VMEM((1, QPAD), F32),
            pltpu.VMEM((1, QPAD), F32),
            pltpu.VMEM((HD, KEYS), BF16),
            pltpu.VMEM((HD, BLOCK), F32),
            pltpu.VMEM((1, BLOCK), F32),
            pltpu.VMEM((4, HD, BLOCK), BF16),
            pltpu.VMEM((4, HD, BLOCK), BF16),
            pltpu.VMEM((4, 8, BLOCK), F32),
            pltpu.VMEM((4, 8, BLOCK), F32),
            pltpu.VMEM((BLOCK, HD), BF16),
            pltpu.VMEM((QPAD, HD), BF16),
            pltpu.VMEM((4, ROWS, OUT), BF16),
            pltpu.VMEM((4, ROWS, OUT), BF16),
            dma((4,)), dma((4,)), dma((4,)),
            dma((4,)), dma((4,)), dma((4,)), dma((4,)), dma((4,)), dma((4,)),
            dma((4 * SOURCES,)), dma((4 * SOURCES,)),
            dma((4,)), dma((4,)), dma((8,)), dma((8,)), dma((16,)), dma((16,)),
            dma((4,)), dma((4,)), dma((4,)), dma((4,)), dma((4,)), dma((4,)),
            dma((4,)), dma((4,)),
        ],
        compiler_params=pltpu.CompilerParams(
            collective_id=1, has_side_effects=True, vmem_limit_bytes=62 * 2**20),
        cost_estimate=pl.CostEstimate(flops=17 * 10**9, bytes_accessed=19 * 10**6, transcendentals=27 * 10**6),
        name="layer",
    )(
        slots, page_counts.reshape(-1), norm_gain.reshape(1, D), hidden_in, w_query, w_keyval.T, w_out,
        kv_store.reshape(16, 4, 2 * PAGE, HD))


def solution(mesh):
    return jax.shard_map(
        local,
        mesh=mesh,
        in_specs=(
            P("pool", None),
            P(),
            P(None, "tp"),
            P(None, "tp"),
            P("tp", None),
            P(("pool", "tp"), None, None, None, None),
            P(None, ("pool", "tp"), None),
            P("pool", None),
        ),
        out_specs=P("pool", "tp"),
        check_vma=False,
    )
```

```python
import math

import jax
import jax.numpy as jnp
from jax import lax
from jax.experimental import pallas as pl
from jax.experimental.pallas import tpu as pltpu
from jax.sharding import PartitionSpec as P

SAMP = 16
MESH = pl.DeviceIdType.MESH
F32 = jnp.float32
BF16 = jnp.bfloat16
PAGE = 128
HD = 128
CAP = 3
D = 8192
LOG2E = 1.4426950408889634
DEAD = 1e30
ROWS = 272
GROUP = 8
SPAN = 128
PAIR = 2 * SPAN
LATE = 144
QROWS = GROUP * ROWS
QPAD = 2304
TILE = 256
FIRST_TILES = (0, 1, 2, 3)
LATER_TILES = (4, 5, 6, 7, 8)
SOURCES = 8
CHUNK = 4
STEPS = 8
KEYS = CHUNK * CAP * PAGE
PART = 512
OUT = 512
NT = (((1,), (1,)), ((), ()))
NN = (((1,), (0,)), ((), ()))
FAR_FIRST = (2, 1, 3)


def plane_offset(i):
    dy = jnp.where(i < 2, 0, jnp.where(i < 6, 1 + 2 * (i % 2), 2))
    dc = jnp.where((i >= 2) & (i < 6), (i - 2) // 2, i % 2)
    return dy, dc


def stage_offset(k):
    return jnp.where(k < 2, k, 5 - k)


def layer_kernel(
    slots_ref, counts_ref, gain_ref, hidden_hbm, wq_hbm, wkv_hbm, wout_hbm, kv_hbm, out_ref,
    hidden, wq, wkv, wout, held0, held1, held2, held3, slots_in, slots_smem,
    ysend, yrecv, squares, q_acc, kv_acc, qown, qall, piece, pieces, turn,
    acc, stat_m, stat_l, vt, turn_o, turn_m, turn_l,
    part_out_a, part_in_a, stat_out_a, stat_in_a, part_out_b, part_in_b, stat_out_b, stat_in_b,
    att_out_a, att_out_b, att_a, att_b, sum_out_a, sum_in_a, sum_out_b, sum_in_b,
    load_sem, wout_load_sem, slot_sem, zk_s, zk_r, zs_s, zs_r, zp_s, zp_r, y_s, y_r,
    xq_s, xq_r, xt_s, xt_r, xw_s, xw_r, xo_s, xo_r, xl_s, xl_r, xa_s, xa_r, zo_s, zo_r,
):
    pool = lax.axis_index("pool")
    tp = lax.axis_index("tp")
    y, c = pool // 2, pool % 2
    z, x = tp // 4, tp % 4
    scale = LOG2E / math.sqrt(HD)
    held = (held0, held1, held2, held3)

    def x_peer(d):
        return (pool, z * 4 + (x + d) % 4)

    def z_peer(d):
        return (pool, ((z + d) % 4) * 4 + x)

    def plane_peer(i):
        dy, dc = plane_offset(i)
        return ((y + dy) % 4) * 2 + (c + dc) % 2

    def remote(src, dst, send_sem, recv_sem, device):
        return pltpu.make_async_remote_copy(
            src_ref=src, dst_ref=dst, send_sem=send_sem, recv_sem=recv_sem, device_id=device, device_id_type=MESH)

    barrier = pltpu.get_barrier_semaphore()
    for i in range(1, SOURCES):
        pl.semaphore_signal(barrier, inc=1, device_id=(plane_peer(i), tp), device_id_type=MESH)
    for d in (1, 2, 3):
        pl.semaphore_signal(barrier, inc=1, device_id=x_peer(d), device_id_type=MESH)
        pl.semaphore_signal(barrier, inc=1, device_id=z_peer(d), device_id_type=MESH)

    own_pages = pltpu.make_async_copy(kv_hbm.at[:, z], held0, load_sem.at[0])
    own_pages.start()
    loads = [
        pltpu.make_async_copy(hidden_hbm, hidden, load_sem.at[1]),
        pltpu.make_async_copy(wq_hbm, wq, load_sem.at[2]),
        pltpu.make_async_copy(wkv_hbm, wkv, load_sem.at[3]),
    ]
    for load in loads:
        load.start()
    own_slots = pltpu.make_async_copy(slots_ref, slots_smem.at[0], slot_sem.at[0])
    own_slots.start()
    pl.semaphore_wait(barrier, SOURCES - 1 + 6)

    def slot_copy(d):
        return remote(slots_ref, slots_in.at[d], zs_s.at[d], zs_r.at[d], z_peer(d))

    def page_copy(d):
        return remote(kv_hbm.at[:, (z + d) % 4], held[d], zk_s.at[d], zk_r.at[d], z_peer(d))

    for d in (1, 3, 2):
        slot_copy(d).start()
    for d in (1, 3):
        page_copy(d).start()

    def y_copy(k, i):
        return remote(
            ysend.at[k, i], yrecv.at[k, i], y_s.at[k * SOURCES + i], y_r.at[k * SOURCES + i], (plane_peer(i), tp))

    def pass_on(k, d):
        for slot in range(CAP):
            yrecv[k, 0, slot] = held[d][slots_smem[d, pool, slot]]

        @pl.loop(1, SOURCES)
        def _(n):
            i = jnp.where(n < SOURCES - 1, n + 1, 1)
            dest = plane_peer(i)
            for slot in range(CAP):
                ysend[k, i, slot] = held[d][slots_smem[d, dest, slot]]
            y_copy(k, i).start()

    own_slots.wait()
    own_pages.wait()
    pass_on(0, 0)

    for load in loads:
        load.wait()
    squares[...] = jnp.zeros_like(squares)

    @pl.loop(0, D // PART)
    def _(n):
        part = hidden[:, pl.ds(pl.multiple_of(n * PART, PART), PART)].astype(F32)
        part = part * part
        for m in range(PART // 128):
            squares[...] += part[:, m * 128:(m + 1) * 128]

    mean = jnp.sum(squares[...], axis=1, keepdims=True) * (1.0 / D)
    squares[...] = jnp.broadcast_to(lax.rsqrt(mean + 1e-05), squares.shape)
    q_acc[...] = jnp.zeros_like(q_acc)
    kv_acc[...] = jnp.zeros_like(kv_acc)

    @pl.loop(0, D // PART)
    def _(n):
        cols = pl.ds(pl.multiple_of(n * PART, PART), PART)
        inverse = squares[:, :1]
        normed = (hidden[:, cols].astype(F32) * inverse * gain_ref[:, cols]).astype(BF16)
        q_acc[...] += jnp.dot(normed, wq[cols, :], preferred_element_type=F32)
        kv_acc[...] += lax.dot_general(normed, wkv[:, cols], NT, preferred_element_type=F32)

    queries = q_acc[...].astype(BF16)
    for h in range(2):
        head = queries[:, h * HD:(h + 1) * HD]
        qown[h * SPAN:(h + 1) * SPAN, :] = head[:SPAN]
        qown[PAIR + h * SPAN:PAIR + (h + 1) * SPAN, :] = head[SPAN:2 * SPAN]
        qown[2 * PAIR + h * SAMP:2 * PAIR + (h + 1) * SAMP, :] = head[2 * SPAN:]

    rows_a = pl.ds(pl.multiple_of(x * PAIR, PAIR), PAIR)
    rows_b = pl.ds(pl.multiple_of(GROUP * SPAN + x * PAIR, PAIR), PAIR)
    rows_c = pl.ds(2 * GROUP * SPAN, GROUP * SAMP)
    own_rows = (rows_a, rows_b, pl.ds(pl.multiple_of(2 * GROUP * SPAN + x * 2 * SAMP, 2 * SAMP), 2 * SAMP))
    made_rows = (pl.ds(0, PAIR), pl.ds(PAIR, PAIR), pl.ds(2 * PAIR, 2 * SAMP))

    def q_copy(d, n):
        return remote(
            qown.at[made_rows[n]], qall.at[own_rows[n]], xq_s.at[d * 3 + n], xq_r.at[d * 3 + n], x_peer(d))

    for n in range(3):
        for d in FAR_FIRST:
            q_copy(d, n).start()
        qall[own_rows[n], :] = qown[made_rows[n], :]
    qall[QROWS:, :] = jnp.zeros((QPAD - QROWS, HD), BF16)

    half = kv_acc[...]
    blank = jnp.zeros_like(half)
    piece[...] = jnp.where(
        x % 2 == 0, jnp.concatenate([half, blank], axis=1), jnp.concatenate([blank, half], axis=1)).astype(BF16)

    def piece_copy(d):
        return remote(piece, pieces.at[z], zp_s.at[d], zp_r.at[d], z_peer(d))

    for d in (1, 2, 3):
        piece_copy(d).start()
    pieces[z] = piece[...]

    def wout_copy(d, n):
        columns = pl.ds(pl.multiple_of((n * 4 + (x + d) % 4) * OUT, OUT), OUT)
        rows = pl.ds(pl.multiple_of(x * 256, 256), 256)
        return remote(wout_hbm.at[:, columns], wout.at[n, rows], xw_s.at[d * 4 + n], xw_r.at[d * 4 + n], x_peer(d))

    def own_wout(n):
        columns = pl.ds(pl.multiple_of((n * 4 + x) * OUT, OUT), OUT)
        rows = pl.ds(pl.multiple_of(x * 256, 256), 256)
        return pltpu.make_async_copy(wout_hbm.at[:, columns], wout.at[n, rows], wout_load_sem.at[n])

    acc[...] = jnp.zeros_like(acc)
    stat_m[...] = jnp.full_like(stat_m, -DEAD)
    stat_l[...] = jnp.zeros_like(stat_l)

    def turn_copy(d, kind):
        return remote(
            pieces.at[kind * 2 + z // 2], turn.at[kind, x], xt_s.at[d * 2 + kind], xt_r.at[d * 2 + kind], x_peer(d))

    def arrived(d, k):
        page_copy(d).wait_recv()
        slot_copy(d).wait_recv()
        to_smem = pltpu.make_async_copy(slots_in.at[d], slots_smem.at[d], slot_sem.at[d])
        to_smem.start()
        to_smem.wait()
        pass_on(k, d)

    arrived(1, 1)
    arrived(3, 2)
    page_copy(2).start()
    for d in (1, 2, 3):
        for n in range(3):
            q_copy(d, n).wait()

    def o_copy(d, part):
        out, into = ((part_out_a, part_in_a), (part_out_b, part_in_b))[part]
        return remote(out.at[d], into.at[d], xo_s.at[d * 2 + part], xo_r.at[d * 2 + part], x_peer(d))

    def l_copy(d, part):
        out, into = ((stat_out_a, stat_in_a), (stat_out_b, stat_in_b))[part]
        return remote(out.at[d], into.at[d], xl_s.at[d * 2 + part], xl_r.at[d * 2 + part], x_peer(d))

    def send_part(part):
        for d in FAR_FIRST:
            start = ((x + d) % 4) * PAIR
            if part == 0:
                cols = pl.ds(pl.multiple_of(start, PAIR), PAIR)
                part_out_a[d] = acc[:, cols].astype(BF16)
                stat_out_a[d, 0:1, :] = stat_m[:, cols]
                stat_out_a[d, 1:2, :] = stat_l[:, cols]
            else:
                cols = pl.ds(pl.multiple_of(GROUP * SPAN + start, PAIR), PAIR)
                part_out_b[d, :, :PAIR] = acc[:, cols].astype(BF16)
                part_out_b[d, :, PAIR:] = acc[:, rows_c].astype(BF16)
                stat_out_b[d, 0:1, :PAIR] = stat_m[:, cols]
                stat_out_b[d, 0:1, PAIR:] = stat_m[:, rows_c]
                stat_out_b[d, 1:2, :PAIR] = stat_l[:, cols]
                stat_out_b[d, 1:2, PAIR:] = stat_l[:, rows_c]
            l_copy(d, part).start()
            o_copy(d, part).start()

    def own_turn():
        for d in (1, 2, 3):
            for kind in range(2):
                turn_copy(d, kind).wait()
        pair = (z % 2) * 2
        turn_keys = turn[0, pair] + turn[0, pair + 1]
        turn_values = turn[1, pair] + turn[1, pair + 1]
        rows = jnp.concatenate([qall[rows_a, :], qall[rows_b, :], qall[rows_c, :]], axis=0)
        count = 2 * PAIR + GROUP * SAMP
        scores = lax.dot_general(turn_keys, rows, NT, preferred_element_type=F32)
        key_idx = lax.broadcasted_iota(jnp.int32, (ROWS, count), 0)
        place = lax.broadcasted_iota(jnp.int32, (ROWS, count), 1)
        token = jnp.where(
            place < PAIR, place % SPAN, jnp.where(place < 2 * PAIR, SPAN + place % SPAN, 2 * SPAN + place % SAMP))
        allowed = (key_idx <= token) & ((key_idx < ROWS - SAMP) | (key_idx == token))
        scores = jnp.where(allowed, scores, -DEAD)
        top = jnp.max(scores, axis=0, keepdims=True)
        probs = jnp.exp2(scores * scale - top * scale)
        turn_m[...] = top
        turn_l[...] = jnp.sum(probs, axis=0, keepdims=True)
        turn_o[...] = lax.dot_general(turn_values.T, probs.astype(BF16), NN, preferred_element_type=F32)

    def visit(n, carry):
        k, first = n // 2, (n % 2) * CHUNK

        @pl.loop(0, CHUNK)
        def _(j):
            @pl.when(first + j > 0)
            def _():
                y_copy(k, first + j).wait_recv()

        live = []
        for j in range(CHUNK):
            dy, dc = plane_offset(first + j)
            holder = (((y + 4 - dy) % 4) * 2 + (c + dc) % 2) * 16 + ((z + 4 - stage_offset(k)) % 4) * 4 + x
            count = counts_ref[holder]
            for slot in range(CAP):
                live.append(count > slot)
        pages = yrecv[k, pl.ds(first, CHUNK)]
        keys = pages[:, :, :PAGE, :].reshape(KEYS, HD)
        vt[...] = pages[:, :, PAGE:, :].reshape(KEYS, HD).T

        def attend(tiles):
            cols = [pl.ds(t * TILE, TILE) for t in tiles]
            all_scores = [lax.dot_general(keys, qall[own, :], NT, preferred_element_type=F32) for own in cols]
            for own, scores in zip(cols, all_scores):
                old_m = stat_m[:, own]
                new_m = old_m
                for j in range(CHUNK * CAP):
                    top = jnp.max(scores[j * PAGE:(j + 1) * PAGE], axis=0, keepdims=True)
                    new_m = jnp.maximum(new_m, jnp.where(live[j], top, -DEAD))
                shift = new_m * scale
                shrink = jnp.exp2(old_m * scale - shift)
                total = stat_l[:, own] * shrink
                weights = []
                for j in range(CHUNK * CAP):
                    probs = jnp.exp2(scores[j * PAGE:(j + 1) * PAGE] * scale - jnp.where(live[j], shift, DEAD))
                    total = total + jnp.sum(probs, axis=0, keepdims=True)
                    weights.append(probs.astype(BF16))
                blended = lax.dot_general(vt[...], jnp.concatenate(weights, axis=0), NN, preferred_element_type=F32)
                acc[:, own] = acc[:, own] * shrink + blended
                stat_m[:, own] = new_m
                stat_l[:, own] = total

        attend(FIRST_TILES)

        @pl.when(n == STEPS - 1)
        def _():
            send_part(0)

        attend(LATER_TILES)

        @pl.when(n == STEPS - 1)
        def _():
            send_part(1)

        @pl.when(n == 0)
        def _():
            for d in (1, 2, 3):
                piece_copy(d).wait()
            for d in FAR_FIRST:
                for kind in range(2):
                    turn_copy(d, kind).start()
            for kind in range(2):
                turn[kind, x] = pieces[kind * 2 + z // 2]
            for d in FAR_FIRST:
                for m in range(4):
                    wout_copy(d, m).start()
            for m in range(4):
                own_wout(m).start()

        @pl.when(n == 3)
        def _():
            arrived(2, 3)

        @pl.when(n == 5)
        def _():
            own_turn()

        return carry

    lax.fori_loop(0, STEPS, visit, 0)

    def merge(own, part, turn_cols):
        into, stats = ((part_in_a, stat_in_a), (part_in_b, stat_in_b))[part]
        for d in (1, 2, 3):
            l_copy(d, part).wait()
            o_copy(d, part).wait()
        tops = [jnp.concatenate([stat_m[:, cols] for cols in own], axis=1) * scale, turn_m[:, turn_cols] * scale]
        sums = [jnp.concatenate([stat_l[:, cols] for cols in own], axis=1), turn_l[:, turn_cols]]
        sources = [jnp.concatenate([acc[:, cols] for cols in own], axis=1), turn_o[:, turn_cols]]
        for d in (1, 2, 3):
            tops.append(stats[d, 0:1, :] * scale)
            sums.append(stats[d, 1:2, :])
            sources.append(into[d].astype(F32))
        top = tops[0]
        for other in tops[1:]:
            top = jnp.maximum(top, other)
        shares = [jnp.exp2(one - top) for one in tops]
        norm = sums[0] * shares[0]
        for one, share in zip(sums[1:], shares[1:]):
            norm = norm + one * share
        inverse = 1.0 / norm
        merged = sources[0] * (shares[0] * inverse)
        for one, share in zip(sources[1:], shares[1:]):
            merged = merged + one * (share * inverse)
        return merged

    def a_copy(d, part):
        out, into = ((att_out_a, att_a), (att_out_b, att_b))[part]
        return remote(out, into.at[rows_a], xa_s.at[d * 2 + part], xa_r.at[d * 2 + part], x_peer(d))

    att_out_a[...] = merge([rows_a], 0, pl.ds(0, PAIR)).T.astype(BF16)
    for d in FAR_FIRST:
        a_copy(d, 0).start()
    att_a[rows_a, :] = att_out_a[...]
    merged = merge([rows_b, rows_c], 1, pl.ds(PAIR, PAIR + GROUP * SAMP)).T.astype(BF16)
    att_out_b[...] = merged[:PAIR]
    for d in FAR_FIRST:
        a_copy(d, 1).start()
    att_b[rows_a, :] = att_out_b[...]
    samples = jnp.concatenate(
        [merged[PAIR + h * SAMP:PAIR + (h + 1) * SAMP] for h in range(GROUP)], axis=1)

    def z_copy(d, part):
        out, into = ((sum_out_a, sum_in_a), (sum_out_b, sum_in_b))[part]
        return remote(out.at[d], into.at[d], zo_s.at[d * 2 + part], zo_r.at[d * 2 + part], z_peer(d))

    for d in (1, 2, 3):
        for m in range(4):
            wout_copy(d, m).wait()
    for m in range(4):
        own_wout(m).wait()

    for d in (1, 2, 3):
        a_copy(d, 0).wait()
    early = jnp.concatenate([att_a[h * SPAN:(h + 1) * SPAN, :] for h in range(GROUP)], axis=1)
    for d in FAR_FIRST:
        sum_out_a[d] = jnp.dot(early, wout[(z + d) % 4], preferred_element_type=F32).astype(BF16)
        z_copy(d, 0).start()
    for d in (1, 2, 3):
        a_copy(d, 1).wait()
    late = jnp.concatenate([att_b[h * SPAN:(h + 1) * SPAN, :] for h in range(GROUP)], axis=1)
    late = jnp.concatenate([late, samples], axis=0)
    for d in FAR_FIRST:
        sum_out_b[d] = jnp.dot(late, wout[(z + d) % 4], preferred_element_type=F32).astype(BF16)
        z_copy(d, 1).start()
    early_out = jnp.dot(early, wout[z], preferred_element_type=F32)
    late_out = jnp.dot(late, wout[z], preferred_element_type=F32)
    for d in (1, 2, 3):
        z_copy(d, 0).wait()
        early_out = early_out + sum_in_a[d].astype(F32)
    out_ref[:SPAN, :] = early_out.astype(BF16)
    for d in (1, 2, 3):
        z_copy(d, 1).wait()
        late_out = late_out + sum_in_b[d].astype(F32)
    out_ref[SPAN:, :] = late_out.astype(BF16)

    for d in (1, 2, 3):
        page_copy(d).wait_send()
        slot_copy(d).wait_send()

    @pl.loop(0, 4)
    def _(k):
        @pl.loop(1, SOURCES)
        def _(i):
            y_copy(k, i).wait_send()


def local(hidden_in, norm_gain, w_query, w_keyval, w_out, kv_store, page_slots, page_counts):
    vmem = pl.BlockSpec(memory_space=pltpu.VMEM)
    smem = pl.BlockSpec(memory_space=pltpu.SMEM)
    anywhere = pl.BlockSpec(memory_space=pl.ANY)
    dma = pltpu.SemaphoreType.DMA
    slots = jnp.pad(page_slots[:, 0, :], ((0, 0), (0, 128 - CAP)))
    return pl.pallas_call(
        layer_kernel,
        out_shape=jax.ShapeDtypeStruct((ROWS, OUT), BF16),
        in_specs=[vmem, smem, vmem, anywhere, anywhere, anywhere, anywhere, anywhere],
        out_specs=vmem,
        scratch_shapes=[
            pltpu.VMEM((ROWS, D), BF16),
            pltpu.VMEM((D, 256), BF16),
            pltpu.VMEM((64, D), BF16),
            pltpu.VMEM((4, 1024, OUT), BF16),
            pltpu.VMEM((16, 2 * PAGE, HD), BF16),
            pltpu.VMEM((16, 2 * PAGE, HD), BF16),
            pltpu.VMEM((16, 2 * PAGE, HD), BF16),
            pltpu.VMEM((16, 2 * PAGE, HD), BF16),
            pltpu.VMEM((4, 8, 128), jnp.int32),
            pltpu.SMEM((4, 8, 128), jnp.int32),
            pltpu.VMEM((4, SOURCES, CAP, 2 * PAGE, HD), BF16),
            pltpu.VMEM((4, SOURCES, CAP, 2 * PAGE, HD), BF16),
            pltpu.VMEM((ROWS, 128), F32),
            pltpu.VMEM((ROWS, 256), F32),
            pltpu.VMEM((ROWS, 64), F32),
            pltpu.VMEM((2 * ROWS, HD), BF16),
            pltpu.VMEM((QPAD, HD), BF16),
            pltpu.VMEM((ROWS, HD), BF16),
            pltpu.VMEM((4, ROWS, HD), BF16),
            pltpu.VMEM((2, 4, ROWS, HD), BF16),
            pltpu.VMEM((HD, QPAD), F32),
            pltpu.VMEM((1, QPAD), F32),
            pltpu.VMEM((1, QPAD), F32),
            pltpu.VMEM((HD, KEYS), BF16),
            pltpu.VMEM((HD, 2 * PAIR + 128), F32),
            pltpu.VMEM((1, 2 * PAIR + 128), F32),
            pltpu.VMEM((1, 2 * PAIR + 128), F32),
            pltpu.VMEM((4, HD, PAIR), BF16),
            pltpu.VMEM((4, HD, PAIR), BF16),
            pltpu.VMEM((4, 8, PAIR), F32),
            pltpu.VMEM((4, 8, PAIR), F32),
            pltpu.VMEM((4, HD, PAIR + 128), BF16),
            pltpu.VMEM((4, HD, PAIR + 128), BF16),
            pltpu.VMEM((4, 8, PAIR + 128), F32),
            pltpu.VMEM((4, 8, PAIR + 128), F32),
            pltpu.VMEM((PAIR, HD), BF16),
            pltpu.VMEM((PAIR, HD), BF16),
            pltpu.VMEM((4 * PAIR, HD), BF16),
            pltpu.VMEM((4 * PAIR, HD), BF16),
            pltpu.VMEM((4, SPAN, OUT), BF16),
            pltpu.VMEM((4, SPAN, OUT), BF16),
            pltpu.VMEM((4, LATE, OUT), BF16),
            pltpu.VMEM((4, LATE, OUT), BF16),
            dma((4,)), dma((4,)), dma((4,)),
            dma((4,)), dma((4,)), dma((4,)), dma((4,)), dma((4,)), dma((4,)),
            dma((4 * SOURCES,)), dma((4 * SOURCES,)),
            dma((12,)), dma((12,)), dma((8,)), dma((8,)), dma((16,)), dma((16,)),
            dma((8,)), dma((8,)), dma((8,)), dma((8,)), dma((8,)), dma((8,)),
            dma((8,)), dma((8,)),
        ],
        compiler_params=pltpu.CompilerParams(
            collective_id=1, has_side_effects=True, vmem_limit_bytes=62 * 2**20),
        cost_estimate=pl.CostEstimate(flops=17 * 10**9, bytes_accessed=19 * 10**6, transcendentals=27 * 10**6),
        name="layer",
    )(
        slots, page_counts.reshape(-1), norm_gain.reshape(1, D), hidden_in, w_query, w_keyval.T, w_out,
        kv_store.reshape(16, 4, 2 * PAGE, HD))


def solution(mesh):
    return jax.shard_map(
        local,
        mesh=mesh,
        in_specs=(
            P("pool", None),
            P(),
            P(None, "tp"),
            P(None, "tp"),
            P("tp", None),
            P(("pool", "tp"), None, None, None, None),
            P(None, ("pool", "tp"), None),
            P("pool", None),
        ),
        out_specs=P("pool", "tp"),
        check_vma=False,
    )
```

```python
import math

import jax
import jax.numpy as jnp
from jax import lax
from jax.experimental import pallas as pl
from jax.experimental.pallas import tpu as pltpu
from jax.sharding import PartitionSpec as P

SAMP = 16
MESH = pl.DeviceIdType.MESH
F32 = jnp.float32
BF16 = jnp.bfloat16
PAGE = 128
HD = 128
CAP = 3
D = 8192
LOG2E = 1.4426950408889634
DEAD = 1e30
ROWS = 272
GROUP = 8
SPAN = 128
PAIR = 2 * SPAN
LATE = 144
QROWS = GROUP * ROWS
QPAD = 2304
TILE = 256
FIRST_TILES = (0, 1, 2, 3)
LATER_TILES = (4, 5, 6, 7, 8)
SOURCES = 8
EARLY_CHUNK = 4
LAST_CHUNK = 2
EARLY_STEPS = 3 * SOURCES // EARLY_CHUNK
LAST_STEPS = SOURCES // LAST_CHUNK
HALF = 256
PART = 512
OUT = 512
NT = (((1,), (1,)), ((), ()))
NN = (((1,), (0,)), ((), ()))
FAR_FIRST = (2, 1, 3)


def plane_offset(i):
    dy = jnp.where(i < 2, 0, jnp.where(i < 6, 1 + 2 * (i % 2), 2))
    dc = jnp.where((i >= 2) & (i < 6), (i - 2) // 2, i % 2)
    return dy, dc


def stage_offset(k):
    return jnp.where(k < 2, k, 5 - k)


def layer_kernel(
    slots_ref, counts_ref, gain_ref, hidden_hbm, wq_hbm, wkv_hbm, wout_hbm, kv_hbm, out_ref,
    hidden, wq, wkv, wout_x, wout_z, held0, keys1, values1, held2, held3, slots_out, slots_in, slots_smem,
    ysend, yrecv, squares, q_acc, kv_acc, qown, qall, piece, pieces, turn,
    acc, stat_m, stat_l, vt, turn_o, turn_m, turn_l,
    part_out_a, part_in_a, stat_out_a, stat_in_a, part_out_b, part_in_b, stat_out_b, stat_in_b,
    att_out_a, att_out_b, samples, att_xa, att_xb, att_za, att_zb,
    sum_out_xa, sum_in_xa, sum_out_xb, sum_in_xb, sum_out_za, sum_in_za, sum_out_zb, sum_in_zb,
    load_sem, wout_load_sem, slot_sem, zk_s, zk_r, zs_s, zs_r, zp_s, zp_r, y_s, y_r,
    xq_s, xq_r, xt_s, xt_r, xw_s, xw_r, zw_s, zw_r,
    xo_s, xo_r, xl_s, xl_r, xa_s, xa_r, za_s, za_r, xo2_s, xo2_r, zo_s, zo_r,
):
    pool = lax.axis_index("pool")
    tp = lax.axis_index("tp")
    y, c = pool // 2, pool % 2
    z, x = tp // 4, tp % 4
    scale = LOG2E / math.sqrt(HD)
    held = (held0, None, held2, held3)

    def x_peer(d):
        return (pool, z * 4 + (x + d) % 4)

    def z_peer(d):
        return (pool, ((z + d) % 4) * 4 + x)

    def plane_peer(i):
        dy, dc = plane_offset(i)
        return ((y + dy) % 4) * 2 + (c + dc) % 2

    def remote(src, dst, send_sem, recv_sem, device):
        return pltpu.make_async_remote_copy(
            src_ref=src, dst_ref=dst, send_sem=send_sem, recv_sem=recv_sem, device_id=device, device_id_type=MESH)

    barrier = pltpu.get_barrier_semaphore()
    for i in range(1, SOURCES):
        pl.semaphore_signal(barrier, inc=1, device_id=(plane_peer(i), tp), device_id_type=MESH)
    for d in (1, 2, 3):
        pl.semaphore_signal(barrier, inc=1, device_id=x_peer(d), device_id_type=MESH)
        pl.semaphore_signal(barrier, inc=1, device_id=z_peer(d), device_id_type=MESH)

    own_pages = pltpu.make_async_copy(kv_hbm.at[:, z], held0, load_sem.at[0])
    own_pages.start()
    loads = [
        pltpu.make_async_copy(hidden_hbm, hidden, load_sem.at[1]),
        pltpu.make_async_copy(wq_hbm, wq, load_sem.at[2]),
        pltpu.make_async_copy(wkv_hbm, wkv, load_sem.at[3]),
    ]
    for load in loads:
        load.start()
    slots_out[:, :CAP] = slots_ref[...]
    own_slots = pltpu.make_async_copy(slots_out, slots_smem.at[0], slot_sem.at[0])
    own_slots.start()
    pl.semaphore_wait(barrier, SOURCES - 1 + 6)

    def slot_copy(d):
        return remote(slots_out, slots_in.at[d], zs_s.at[d], zs_r.at[d], z_peer(d))

    def page_copy(d):
        return remote(kv_hbm.at[:, (z + d) % 4], held[d], zk_s.at[d], zk_r.at[d], z_peer(d))

    def half_copy(half):
        into = (keys1, values1)[half]
        source = kv_hbm.at[:, (z + 1) % 4, pl.ds(half * PAGE, PAGE)]
        return remote(source, into, zk_s.at[half], zk_r.at[half], z_peer(1))

    for d in (1, 3, 2):
        slot_copy(d).start()
    half_copy(0).start()
    page_copy(3).start()

    def y_copy(k, i):
        return remote(
            ysend.at[k, i], yrecv.at[k, i], y_s.at[k * SOURCES + i], y_r.at[k * SOURCES + i], (plane_peer(i), tp))

    def half_y_copy(half, i):
        rows = pl.ds(half * PAGE, PAGE)
        own = (1 + 3 * half) * SOURCES + i
        return remote(
            ysend.at[1, i, :, rows], yrecv.at[1, i, :, rows], y_s.at[own], y_r.at[own], (plane_peer(i), tp))

    def pass_on(k, d):
        for slot in range(CAP):
            yrecv[k, 0, slot] = held[d][slots_smem[d, pool, slot]]

        @pl.loop(1, SOURCES)
        def _(i):
            dest = plane_peer(i)
            for slot in range(CAP):
                ysend[k, i, slot] = held[d][slots_smem[d, dest, slot]]
            y_copy(k, i).start()

    def pass_half(half):
        pages = (keys1, values1)[half]
        rows = pl.ds(half * PAGE, PAGE)
        for slot in range(CAP):
            yrecv[1, 0, slot, rows] = pages[slots_smem[1, pool, slot]]

        @pl.loop(1, SOURCES)
        def _(i):
            dest = plane_peer(i)
            for slot in range(CAP):
                ysend[1, i, slot, rows] = pages[slots_smem[1, dest, slot]]
            half_y_copy(half, i).start()

    own_slots.wait()
    own_pages.wait()
    pass_on(0, 0)

    for load in loads:
        load.wait()
    squares[...] = jnp.zeros_like(squares)

    @pl.loop(0, D // PART)
    def _(n):
        part = hidden[:, pl.ds(pl.multiple_of(n * PART, PART), PART)].astype(F32)
        part = part * part
        for m in range(PART // 128):
            squares[...] += part[:, m * 128:(m + 1) * 128]

    half_copy(1).start()
    mean = jnp.sum(squares[...], axis=1, keepdims=True) * (1.0 / D)
    squares[...] = jnp.broadcast_to(lax.rsqrt(mean + 1e-05), squares.shape)
    q_acc[...] = jnp.zeros_like(q_acc)
    kv_acc[...] = jnp.zeros_like(kv_acc)

    @pl.loop(0, D // PART)
    def _(n):
        cols = pl.ds(pl.multiple_of(n * PART, PART), PART)
        inverse = squares[:, :1]
        normed = (hidden[:, cols].astype(F32) * inverse * gain_ref[:, cols]).astype(BF16)
        q_acc[...] += jnp.dot(normed, wq[cols, :], preferred_element_type=F32)
        kv_acc[...] += lax.dot_general(normed, wkv[:, cols], NT, preferred_element_type=F32)

    queries = q_acc[...].astype(BF16)
    for h in range(2):
        head = queries[:, h * HD:(h + 1) * HD]
        qown[h * SPAN:(h + 1) * SPAN, :] = head[:SPAN]
        qown[PAIR + h * SPAN:PAIR + (h + 1) * SPAN, :] = head[SPAN:2 * SPAN]
        qown[2 * PAIR + h * SAMP:2 * PAIR + (h + 1) * SAMP, :] = head[2 * SPAN:]

    rows_a = pl.ds(pl.multiple_of(x * PAIR, PAIR), PAIR)
    rows_b = pl.ds(pl.multiple_of(GROUP * SPAN + x * PAIR, PAIR), PAIR)
    rows_c = pl.ds(2 * GROUP * SPAN, GROUP * SAMP)
    own_rows = (rows_a, rows_b, pl.ds(pl.multiple_of(2 * GROUP * SPAN + x * 2 * SAMP, 2 * SAMP), 2 * SAMP))
    made_rows = (pl.ds(0, PAIR), pl.ds(PAIR, PAIR), pl.ds(2 * PAIR, 2 * SAMP))

    def q_copy(d, n):
        return remote(
            qown.at[made_rows[n]], qall.at[own_rows[n]], xq_s.at[d * 3 + n], xq_r.at[d * 3 + n], x_peer(d))

    for n in range(3):
        for d in FAR_FIRST:
            q_copy(d, n).start()
        qall[own_rows[n], :] = qown[made_rows[n], :]
    qall[QROWS:, :] = jnp.zeros((QPAD - QROWS, HD), BF16)

    half = kv_acc[...]
    blank = jnp.zeros_like(half)
    piece[...] = jnp.where(
        x % 2 == 0, jnp.concatenate([half, blank], axis=1), jnp.concatenate([blank, half], axis=1)).astype(BF16)

    def piece_copy(d):
        return remote(piece, pieces.at[z], zp_s.at[d], zp_r.at[d], z_peer(d))

    for d in (1, 2, 3):
        piece_copy(d).start()
    pieces[z] = piece[...]

    def wout_columns(to_z, to_x, half):
        return pl.ds(pl.multiple_of((to_z * 4 + to_x) * OUT + half * HALF, HALF), HALF)

    def line_rows(place):
        return pl.ds(pl.multiple_of(place * 256, 256), 256)

    def wout_x_copy(d, n):
        part = 2 * c + n
        return remote(
            wout_hbm.at[:, wout_columns(part, (x + d) % 4, 0)], wout_x.at[part, line_rows(x)],
            xw_s.at[d * 2 + n], xw_r.at[d * 2 + n], x_peer(d))

    def wout_z_copy(d, n):
        part = 2 * c + n
        return remote(
            wout_hbm.at[:, wout_columns((z + d) % 4, part, 1)], wout_z.at[part, line_rows(z)],
            zw_s.at[d * 2 + n], zw_r.at[d * 2 + n], z_peer(d))

    def own_wout_x(n):
        part = 2 * c + n
        return pltpu.make_async_copy(
            wout_hbm.at[:, wout_columns(part, x, 0)], wout_x.at[part, line_rows(x)], wout_load_sem.at[n])

    def own_wout_z(n):
        part = 2 * c + n
        return pltpu.make_async_copy(
            wout_hbm.at[:, wout_columns(z, part, 1)], wout_z.at[part, line_rows(z)], wout_load_sem.at[2 + n])

    def wout_x_share(n):
        part = 2 * c + n
        return remote(wout_x.at[part], wout_x.at[part], xw_s.at[n], xw_r.at[n], (y * 2 + 1 - c, tp))

    def wout_z_share(n):
        part = 2 * c + n
        return remote(wout_z.at[part], wout_z.at[part], zw_s.at[n], zw_r.at[n], (y * 2 + 1 - c, tp))

    acc[...] = jnp.zeros_like(acc)
    stat_m[...] = jnp.full_like(stat_m, -DEAD)
    stat_l[...] = jnp.zeros_like(stat_l)

    def turn_copy(d, kind):
        return remote(
            pieces.at[kind * 2 + z // 2], turn.at[kind, x], xt_s.at[d * 2 + kind], xt_r.at[d * 2 + kind], x_peer(d))

    def numbers_arrived(d):
        slot_copy(d).wait_recv()
        to_smem = pltpu.make_async_copy(slots_in.at[d], slots_smem.at[d], slot_sem.at[d])
        to_smem.start()
        to_smem.wait()

    def arrived(d, k):
        page_copy(d).wait_recv()
        numbers_arrived(d)
        pass_on(k, d)

    for d in (1, 2, 3):
        for n in range(3):
            q_copy(d, n).wait()

    def o_copy(d, part):
        out, into = ((part_out_a, part_in_a), (part_out_b, part_in_b))[part]
        return remote(out.at[d], into.at[d], xo_s.at[d * 2 + part], xo_r.at[d * 2 + part], x_peer(d))

    def l_copy(d, part):
        out, into = ((stat_out_a, stat_in_a), (stat_out_b, stat_in_b))[part]
        return remote(out.at[d], into.at[d], xl_s.at[d * 2 + part], xl_r.at[d * 2 + part], x_peer(d))

    def send_part(part):
        for d in FAR_FIRST:
            start = ((x + d) % 4) * PAIR
            if part == 0:
                cols = pl.ds(pl.multiple_of(start, PAIR), PAIR)
                part_out_a[d] = acc[:, cols].astype(BF16)
                stat_out_a[d, 0:1, :] = stat_m[:, cols]
                stat_out_a[d, 1:2, :] = stat_l[:, cols]
            else:
                cols = pl.ds(pl.multiple_of(GROUP * SPAN + start, PAIR), PAIR)
                part_out_b[d, :, :PAIR] = acc[:, cols].astype(BF16)
                part_out_b[d, :, PAIR:] = acc[:, rows_c].astype(BF16)
                stat_out_b[d, 0:1, :PAIR] = stat_m[:, cols]
                stat_out_b[d, 0:1, PAIR:] = stat_m[:, rows_c]
                stat_out_b[d, 1:2, :PAIR] = stat_l[:, cols]
                stat_out_b[d, 1:2, PAIR:] = stat_l[:, rows_c]
            l_copy(d, part).start()
            o_copy(d, part).start()

    def own_turn():
        for d in (1, 2, 3):
            for kind in range(2):
                turn_copy(d, kind).wait()
        pair = (z % 2) * 2
        turn_keys = turn[0, pair] + turn[0, pair + 1]
        turn_values = turn[1, pair] + turn[1, pair + 1]
        rows = jnp.concatenate([qall[rows_a, :], qall[rows_b, :], qall[rows_c, :]], axis=0)
        count = 2 * PAIR + GROUP * SAMP
        scores = lax.dot_general(turn_keys, rows, NT, preferred_element_type=F32)
        key_idx = lax.broadcasted_iota(jnp.int32, (ROWS, count), 0)
        place = lax.broadcasted_iota(jnp.int32, (ROWS, count), 1)
        token = jnp.where(
            place < PAIR, place % SPAN, jnp.where(place < 2 * PAIR, SPAN + place % SPAN, 2 * SPAN + place % SAMP))
        allowed = (key_idx <= token) & ((key_idx < ROWS - SAMP) | (key_idx == token))
        scores = jnp.where(allowed, scores, -DEAD)
        top = jnp.max(scores, axis=0, keepdims=True)
        probs = jnp.exp2(scores * scale - top * scale)
        turn_m[...] = top
        turn_l[...] = jnp.sum(probs, axis=0, keepdims=True)
        turn_o[...] = lax.dot_general(turn_values.T, probs.astype(BF16), NN, preferred_element_type=F32)

    def attend(k, first, chunk, between=None):
        slots = chunk * CAP

        @pl.loop(0, chunk)
        def _(j):
            @pl.when((first + j > 0) & (k != 1))
            def _():
                y_copy(k, first + j).wait_recv()

            @pl.when((first + j > 0) & (k == 1))
            def _():
                half_y_copy(0, first + j).wait_recv()
                half_y_copy(1, first + j).wait_recv()

        live = []
        for j in range(chunk):
            dy, dc = plane_offset(first + j)
            holder = (((y + 4 - dy) % 4) * 2 + (c + dc) % 2) * 16 + ((z + 4 - stage_offset(k)) % 4) * 4 + x
            count = counts_ref[holder]
            for slot in range(CAP):
                live.append(count > slot)
        pages = yrecv[k, pl.ds(first, chunk)]
        keys = pages[:, :, :PAGE, :].reshape(slots * PAGE, HD)
        width = pl.ds(0, slots * PAGE)
        vt[:, width] = pages[:, :, PAGE:, :].reshape(slots * PAGE, HD).T

        def some(tiles):
            cols = [pl.ds(t * TILE, TILE) for t in tiles]
            all_scores = [lax.dot_general(keys, qall[own, :], NT, preferred_element_type=F32) for own in cols]
            for own, scores in zip(cols, all_scores):
                old_m = stat_m[:, own]
                new_m = old_m
                for j in range(slots):
                    top = jnp.max(scores[j * PAGE:(j + 1) * PAGE], axis=0, keepdims=True)
                    new_m = jnp.maximum(new_m, jnp.where(live[j], top, -DEAD))
                shift = new_m * scale
                shrink = jnp.exp2(old_m * scale - shift)
                total = stat_l[:, own] * shrink
                weights = []
                for j in range(slots):
                    probs = jnp.exp2(scores[j * PAGE:(j + 1) * PAGE] * scale - jnp.where(live[j], shift, DEAD))
                    total = total + jnp.sum(probs, axis=0, keepdims=True)
                    weights.append(probs.astype(BF16))
                blended = lax.dot_general(
                    vt[:, width], jnp.concatenate(weights, axis=0), NN, preferred_element_type=F32)
                acc[:, own] = acc[:, own] * shrink + blended
                stat_m[:, own] = new_m
                stat_l[:, own] = total

        some(FIRST_TILES)
        if between is not None:
            between()
        some(LATER_TILES)

    def early_step(n, carry):
        attend(n // 2, (n % 2) * EARLY_CHUNK, EARLY_CHUNK)

        @pl.when(n == 0)
        def _():
            numbers_arrived(1)
            half_copy(0).wait_recv()
            pass_half(0)

        @pl.when(n == 1)
        def _():
            half_copy(1).wait_recv()
            pass_half(1)
            arrived(3, 2)
            page_copy(2).start()
            for d in (1, 2, 3):
                piece_copy(d).wait()
            for d in FAR_FIRST:
                for kind in range(2):
                    turn_copy(d, kind).start()
            for kind in range(2):
                turn[kind, x] = pieces[kind * 2 + z // 2]
            for d in FAR_FIRST:
                for m in range(2):
                    wout_x_copy(d, m).start()
            for m in range(2):
                own_wout_x(m).start()
                own_wout_z(m).start()

        @pl.when(n == 2)
        def _():
            own_turn()

        @pl.when(n == 3)
        def _():
            arrived(2, 3)
            for d in FAR_FIRST:
                for m in range(2):
                    wout_z_copy(d, m).start()

        return carry

    def last_step(n, carry):
        def when_last(part):
            @pl.when(n == LAST_STEPS - 1)
            def _():
                send_part(part)

        attend(3, n * LAST_CHUNK, LAST_CHUNK, lambda: when_last(0))
        when_last(1)

        @pl.when(n == 0)
        def _():
            for m in range(2):
                for d in (1, 2, 3):
                    wout_x_copy(d, m).wait()
                own_wout_x(m).wait()
                wout_x_share(m).start()

        @pl.when(n == 1)
        def _():
            for m in range(2):
                for d in (1, 2, 3):
                    wout_z_copy(d, m).wait()
                own_wout_z(m).wait()
                wout_z_share(m).start()

        return carry

    lax.fori_loop(0, EARLY_STEPS, early_step, 0)
    lax.fori_loop(0, LAST_STEPS, last_step, 0)

    def merge(own, part, turn_cols):
        into, stats = ((part_in_a, stat_in_a), (part_in_b, stat_in_b))[part]
        for d in (1, 2, 3):
            l_copy(d, part).wait()
            o_copy(d, part).wait()
        tops = [jnp.concatenate([stat_m[:, cols] for cols in own], axis=1) * scale, turn_m[:, turn_cols] * scale]
        sums = [jnp.concatenate([stat_l[:, cols] for cols in own], axis=1), turn_l[:, turn_cols]]
        sources = [jnp.concatenate([acc[:, cols] for cols in own], axis=1), turn_o[:, turn_cols]]
        for d in (1, 2, 3):
            tops.append(stats[d, 0:1, :] * scale)
            sums.append(stats[d, 1:2, :])
            sources.append(into[d].astype(F32))
        top = tops[0]
        for other in tops[1:]:
            top = jnp.maximum(top, other)
        shares = [jnp.exp2(one - top) for one in tops]
        norm = sums[0] * shares[0]
        for one, share in zip(sums[1:], shares[1:]):
            norm = norm + one * share
        inverse = 1.0 / norm
        merged = sources[0] * (shares[0] * inverse)
        for one, share in zip(sources[1:], shares[1:]):
            merged = merged + one * (share * inverse)
        return merged

    def ax_copy(d, part):
        out, into = ((att_out_a, att_xa), (att_out_b, att_xb))[part]
        return remote(
            out.at[pl.ds(0, PAIR)], into.at[rows_a], xa_s.at[d * 2 + part], xa_r.at[d * 2 + part], x_peer(d))

    def az_copy(d, part):
        out, into = ((att_out_a, att_za), (att_out_b, att_zb))[part]
        return remote(out, into.at[z], za_s.at[d * 2 + part], za_r.at[d * 2 + part], z_peer(d))

    att_out_a[...] = merge([rows_a], 0, pl.ds(0, PAIR)).T.astype(BF16)
    for d in FAR_FIRST:
        ax_copy(d, 0).start()
        az_copy(d, 0).start()
    att_xa[rows_a, :] = att_out_a[...]
    att_za[z] = att_out_a[...]
    merged = merge([rows_b, rows_c], 1, pl.ds(PAIR, PAIR + GROUP * SAMP)).T.astype(BF16)
    samples[...] = merged[PAIR:]
    att_out_b[:PAIR, :] = merged[:PAIR]
    att_out_b[PAIR:, :] = samples[pl.ds(pl.multiple_of(x * 2 * SAMP, 2 * SAMP), 2 * SAMP), :]
    for d in FAR_FIRST:
        ax_copy(d, 1).start()
        az_copy(d, 1).start()
    att_xb[rows_a, :] = att_out_b[:PAIR, :]
    att_zb[z] = att_out_b[...]

    def sum_z_copy(d, part):
        out, into = ((sum_out_za, sum_in_za), (sum_out_zb, sum_in_zb))[part]
        return remote(out.at[d], into.at[d], zo_s.at[d * 2 + part], zo_r.at[d * 2 + part], z_peer(d))

    def sum_x_copy(d, part):
        out, into = ((sum_out_xa, sum_in_xa), (sum_out_xb, sum_in_xb))[part]
        return remote(out.at[d], into.at[d], xo2_s.at[d * 2 + part], xo2_r.at[d * 2 + part], x_peer(d))

    def project(part, attended_x, attended_z):
        out_x, out_z = ((sum_out_xa, sum_out_za), (sum_out_xb, sum_out_zb))[part]
        for d in FAR_FIRST:
            out_z[d] = jnp.dot(attended_x, wout_x[(z + d) % 4], preferred_element_type=F32).astype(BF16)
            sum_z_copy(d, part).start()
            out_x[d] = jnp.dot(attended_z, wout_z[(x + d) % 4], preferred_element_type=F32).astype(BF16)
            sum_x_copy(d, part).start()

    def line_up(ref, start, size):
        return jnp.concatenate(
            [ref[m, start + h * size:start + (h + 1) * size, :] for m in range(4) for h in range(2)], axis=1)

    for m in range(2):
        wout_x_share(m).wait()
        wout_z_share(m).wait()
    for d in (1, 2, 3):
        ax_copy(d, 0).wait()
        az_copy(d, 0).wait()
    early_x = jnp.concatenate([att_xa[h * SPAN:(h + 1) * SPAN, :] for h in range(GROUP)], axis=1)
    early_z = line_up(att_za, 0, SPAN)
    project(0, early_x, early_z)
    for d in (1, 2, 3):
        ax_copy(d, 1).wait()
        az_copy(d, 1).wait()
    late_x = jnp.concatenate(
        [
            jnp.concatenate([att_xb[h * SPAN:(h + 1) * SPAN, :] for h in range(GROUP)], axis=1),
            jnp.concatenate([samples[h * SAMP:(h + 1) * SAMP, :] for h in range(GROUP)], axis=1),
        ],
        axis=0)
    late_z = jnp.concatenate([line_up(att_zb, 0, SPAN), line_up(att_zb, PAIR, SAMP)], axis=0)
    project(1, late_x, late_z)
    sums_z = [jnp.dot(one, wout_x[z], preferred_element_type=F32) for one in (early_x, late_x)]
    sums_x = [jnp.dot(one, wout_z[x], preferred_element_type=F32) for one in (early_z, late_z)]
    for part, rows in ((0, slice(0, SPAN)), (1, slice(SPAN, ROWS))):
        sum_x, sum_z = sums_x[part], sums_z[part]
        in_x, in_z = ((sum_in_xa, sum_in_za), (sum_in_xb, sum_in_zb))[part]
        for d in (1, 2, 3):
            sum_z_copy(d, part).wait()
            sum_z = sum_z + in_z[d].astype(F32)
            sum_x_copy(d, part).wait()
            sum_x = sum_x + in_x[d].astype(F32)
        out_ref[rows, :HALF] = sum_z.astype(BF16)
        out_ref[rows, HALF:] = sum_x.astype(BF16)

    for d in (1, 2, 3):
        slot_copy(d).wait_send()
    for d in (2, 3):
        page_copy(d).wait_send()
    for half in range(2):
        half_copy(half).wait_send()

    @pl.loop(0, 4)
    def _(k):
        @pl.loop(1, SOURCES)
        def _(i):
            @pl.when(k != 1)
            def _():
                y_copy(k, i).wait_send()

            @pl.when(k == 1)
            def _():
                half_y_copy(0, i).wait_send()
                half_y_copy(1, i).wait_send()


def local(hidden_in, norm_gain, w_query, w_keyval, w_out, kv_store, page_slots, page_counts):
    vmem = pl.BlockSpec(memory_space=pltpu.VMEM)
    smem = pl.BlockSpec(memory_space=pltpu.SMEM)
    anywhere = pl.BlockSpec(memory_space=pl.ANY)
    dma = pltpu.SemaphoreType.DMA
    slots = page_slots[:, 0, :]
    return pl.pallas_call(
        layer_kernel,
        out_shape=jax.ShapeDtypeStruct((ROWS, OUT), BF16),
        in_specs=[vmem, smem, vmem, anywhere, anywhere, anywhere, anywhere, anywhere],
        out_specs=vmem,
        scratch_shapes=[
            pltpu.VMEM((ROWS, D), BF16),
            pltpu.VMEM((D, 256), BF16),
            pltpu.VMEM((64, D), BF16),
            pltpu.VMEM((4, 1024, HALF), BF16),
            pltpu.VMEM((4, 1024, HALF), BF16),
            pltpu.VMEM((16, 2 * PAGE, HD), BF16),
            pltpu.VMEM((16, PAGE, HD), BF16),
            pltpu.VMEM((16, PAGE, HD), BF16),
            pltpu.VMEM((16, 2 * PAGE, HD), BF16),
            pltpu.VMEM((16, 2 * PAGE, HD), BF16),
            pltpu.VMEM((8, 128), jnp.int32),
            pltpu.VMEM((4, 8, 128), jnp.int32),
            pltpu.SMEM((4, 8, 128), jnp.int32),
            pltpu.VMEM((4, SOURCES, CAP, 2 * PAGE, HD), BF16),
            pltpu.VMEM((4, SOURCES, CAP, 2 * PAGE, HD), BF16),
            pltpu.VMEM((ROWS, 128), F32),
            pltpu.VMEM((ROWS, 256), F32),
            pltpu.VMEM((ROWS, 64), F32),
            pltpu.VMEM((2 * ROWS, HD), BF16),
            pltpu.VMEM((QPAD, HD), BF16),
            pltpu.VMEM((ROWS, HD), BF16),
            pltpu.VMEM((4, ROWS, HD), BF16),
            pltpu.VMEM((2, 4, ROWS, HD), BF16),
            pltpu.VMEM((HD, QPAD), F32),
            pltpu.VMEM((1, QPAD), F32),
            pltpu.VMEM((1, QPAD), F32),
            pltpu.VMEM((HD, EARLY_CHUNK * CAP * PAGE), BF16),
            pltpu.VMEM((HD, 2 * PAIR + 128), F32),
            pltpu.VMEM((1, 2 * PAIR + 128), F32),
            pltpu.VMEM((1, 2 * PAIR + 128), F32),
            pltpu.VMEM((4, HD, PAIR), BF16),
            pltpu.VMEM((4, HD, PAIR), BF16),
            pltpu.VMEM((4, 8, PAIR), F32),
            pltpu.VMEM((4, 8, PAIR), F32),
            pltpu.VMEM((4, HD, PAIR + 128), BF16),
            pltpu.VMEM((4, HD, PAIR + 128), BF16),
            pltpu.VMEM((4, 8, PAIR + 128), F32),
            pltpu.VMEM((4, 8, PAIR + 128), F32),
            pltpu.VMEM((PAIR, HD), BF16),
            pltpu.VMEM((PAIR + 2 * SAMP, HD), BF16),
            pltpu.VMEM((GROUP * SAMP, HD), BF16),
            pltpu.VMEM((4 * PAIR, HD), BF16),
            pltpu.VMEM((4 * PAIR, HD), BF16),
            pltpu.VMEM((4, PAIR, HD), BF16),
            pltpu.VMEM((4, PAIR + 2 * SAMP, HD), BF16),
            pltpu.VMEM((4, SPAN, HALF), BF16),
            pltpu.VMEM((4, SPAN, HALF), BF16),
            pltpu.VMEM((4, LATE, HALF), BF16),
            pltpu.VMEM((4, LATE, HALF), BF16),
            pltpu.VMEM((4, SPAN, HALF), BF16),
            pltpu.VMEM((4, SPAN, HALF), BF16),
            pltpu.VMEM((4, LATE, HALF), BF16),
            pltpu.VMEM((4, LATE, HALF), BF16),
            dma((4,)), dma((4,)), dma((4,)),
            dma((4,)), dma((4,)), dma((4,)), dma((4,)), dma((4,)), dma((4,)),
            dma((5 * SOURCES,)), dma((5 * SOURCES,)),
            dma((12,)), dma((12,)), dma((8,)), dma((8,)), dma((8,)), dma((8,)),
            dma((8,)), dma((8,)),
            dma((8,)), dma((8,)), dma((8,)), dma((8,)), dma((8,)), dma((8,)),
            dma((8,)), dma((8,)), dma((8,)), dma((8,)), dma((8,)), dma((8,)),
        ],
        compiler_params=pltpu.CompilerParams(
            collective_id=1, has_side_effects=True, vmem_limit_bytes=62 * 2**20),
        cost_estimate=pl.CostEstimate(flops=17 * 10**9, bytes_accessed=19 * 10**6, transcendentals=27 * 10**6),
        name="layer",
    )(
        slots, page_counts.reshape(-1), norm_gain.reshape(1, D), hidden_in, w_query, w_keyval.T, w_out,
        kv_store.reshape(16, 4, 2 * PAGE, HD))


def solution(mesh):
    return jax.shard_map(
        local,
        mesh=mesh,
        in_specs=(
            P("pool", None),
            P(),
            P(None, "tp"),
            P(None, "tp"),
            P("tp", None),
            P(("pool", "tp"), None, None, None, None),
            P(None, ("pool", "tp"), None),
            P("pool", None),
        ),
        out_specs=P("pool", "tp"),
        check_vma=False,
    )
```

```python
import math

import jax
import jax.numpy as jnp
from jax import lax
from jax.experimental import pallas as pl
from jax.experimental.pallas import tpu as pltpu
from jax.sharding import PartitionSpec as P

SAMP = 16
MESH = pl.DeviceIdType.MESH
F32 = jnp.float32
BF16 = jnp.bfloat16
PAGE = 128
HD = 128
CAP = 3
D = 8192
LOG2E = 1.4426950408889634
DEAD = 1e30
ROWS = 272
GROUP = 8
SPAN = 128
PAIR = 2 * SPAN
EARLY = 144
QROWS = GROUP * ROWS
QPAD = 2304
TILE = 256
FIRST_TILES = (0, 1, 2, 3, 8)
LATER_TILES = (4, 5, 6, 7)
SOURCES = 8
EARLY_CHUNK = 4
LAST_CHUNK = 2
EARLY_STEPS = 3 * SOURCES // EARLY_CHUNK
LAST_STEPS = SOURCES // LAST_CHUNK
HALF = 256
PART = 512
OUT = 512
NT = (((1,), (1,)), ((), ()))
NN = (((1,), (0,)), ((), ()))
FAR_FIRST = (2, 1, 3)


def plane_offset(i):
    dy = jnp.where(i < 2, 0, jnp.where(i < 6, 1 + 2 * (i % 2), 2))
    dc = jnp.where((i >= 2) & (i < 6), (i - 2) // 2, i % 2)
    return dy, dc


def stage_offset(k):
    return jnp.where(k < 2, k, 5 - k)


def layer_kernel(
    slots_hbm, counts_hbm, gain_hbm, hidden_hbm, wq_hbm, wkv_hbm, wout_hbm, kv_hbm, out_ref,
    counts_ref, gain_ref, slots_own, hidden, wq, wkv, wout_x, wout_z, held0, keys1, values1, held2, held3, slots_out, slots_in, slots_smem,
    ysend, yrecv, squares, q_acc, kv_acc, qown, qall, piece, pieces, turn,
    acc, stat_m, stat_l, vt, turn_o, turn_m, turn_l,
    part_out_a, part_in_a, stat_out_a, stat_in_a, part_out_b, part_in_b, stat_out_b, stat_in_b,
    att_out_a, att_out_b, samples, att_xa, att_xb, att_za, att_zb,
    sum_out_xa, sum_in_xa, sum_out_xb, sum_in_xb, sum_out_za, sum_in_za, sum_out_zb, sum_in_zb,
    load_sem, wout_load_sem, slot_sem, zk_s, zk_r, zs_s, zs_r, zp_s, zp_r, y_s, y_r,
    xq_s, xq_r, xt_s, xt_r, xw_s, xw_r, zw_s, zw_r,
    xo_s, xo_r, xl_s, xl_r, xa_s, xa_r, za_s, za_r, xo2_s, xo2_r, zo_s, zo_r,
):
    pool = lax.axis_index("pool")
    tp = lax.axis_index("tp")
    y, c = pool // 2, pool % 2
    z, x = tp // 4, tp % 4
    scale = LOG2E / math.sqrt(HD)
    held = (held0, None, held2, held3)

    def x_peer(d):
        return (pool, z * 4 + (x + d) % 4)

    def z_peer(d):
        return (pool, ((z + d) % 4) * 4 + x)

    def plane_peer(i):
        dy, dc = plane_offset(i)
        return ((y + dy) % 4) * 2 + (c + dc) % 2

    def remote(src, dst, send_sem, recv_sem, device):
        return pltpu.make_async_remote_copy(
            src_ref=src, dst_ref=dst, send_sem=send_sem, recv_sem=recv_sem, device_id=device, device_id_type=MESH)

    own_pages = pltpu.make_async_copy(kv_hbm.at[:, z], held0, load_sem.at[0])
    own_pages.start()
    fetch_slots = pltpu.make_async_copy(slots_hbm, slots_own, load_sem.at[4])
    fetch_slots.start()
    loads = [
        pltpu.make_async_copy(hidden_hbm, hidden, load_sem.at[1]),
        pltpu.make_async_copy(wq_hbm, wq, load_sem.at[2]),
        pltpu.make_async_copy(wkv_hbm, wkv, load_sem.at[3]),
        pltpu.make_async_copy(gain_hbm, gain_ref, load_sem.at[5]),
        pltpu.make_async_copy(counts_hbm, counts_ref, load_sem.at[6]),
    ]
    barrier = pltpu.get_barrier_semaphore()
    for i in range(1, SOURCES):
        pl.semaphore_signal(barrier, inc=1, device_id=(plane_peer(i), tp), device_id_type=MESH)
    for d in (1, 2, 3):
        pl.semaphore_signal(barrier, inc=1, device_id=x_peer(d), device_id_type=MESH)
        pl.semaphore_signal(barrier, inc=1, device_id=z_peer(d), device_id_type=MESH)

    for load in loads:
        load.start()
    fetch_slots.wait()
    for slot in range(CAP):
        slots_out[slot:slot + 1, :8] = slots_own[slot]
    own_slots = pltpu.make_async_copy(slots_out, slots_smem.at[0], slot_sem.at[0])
    own_slots.start()
    pl.semaphore_wait(barrier, SOURCES - 1 + 6)

    def slot_copy(d):
        return remote(slots_out, slots_in.at[d], zs_s.at[d], zs_r.at[d], z_peer(d))

    def page_copy(d):
        return remote(kv_hbm.at[:, (z + d) % 4], held[d], zk_s.at[d], zk_r.at[d], z_peer(d))

    def half_copy(half):
        into = (keys1, values1)[half]
        source = kv_hbm.at[:, (z + 1) % 4, pl.ds(half * PAGE, PAGE)]
        return remote(source, into, zk_s.at[half], zk_r.at[half], z_peer(1))

    for d in (1, 3, 2):
        slot_copy(d).start()
    half_copy(0).start()
    page_copy(3).start()

    def y_copy(k, i):
        return remote(
            ysend.at[k, i], yrecv.at[k, i], y_s.at[k * SOURCES + i], y_r.at[k * SOURCES + i], (plane_peer(i), tp))

    def half_y_copy(half, i):
        rows = pl.ds(half * PAGE, PAGE)
        own = (1 + 3 * half) * SOURCES + i
        return remote(
            ysend.at[1, i, :, rows], yrecv.at[1, i, :, rows], y_s.at[own], y_r.at[own], (plane_peer(i), tp))

    def pass_on(k, d):
        for slot in range(CAP):
            yrecv[k, 0, slot] = held[d][slots_smem[d, slot, pool]]

        @pl.loop(1, SOURCES)
        def _(i):
            dest = plane_peer(i)
            for slot in range(CAP):
                ysend[k, i, slot] = held[d][slots_smem[d, slot, dest]]
            y_copy(k, i).start()

    def pass_half(half):
        pages = (keys1, values1)[half]
        rows = pl.ds(half * PAGE, PAGE)
        for slot in range(CAP):
            yrecv[1, 0, slot, rows] = pages[slots_smem[1, slot, pool]]

        @pl.loop(1, SOURCES)
        def _(i):
            dest = plane_peer(i)
            for slot in range(CAP):
                ysend[1, i, slot, rows] = pages[slots_smem[1, slot, dest]]
            half_y_copy(half, i).start()

    own_slots.wait()
    own_pages.wait()
    pass_on(0, 0)

    for load in loads:
        load.wait()
    squares[...] = jnp.zeros_like(squares)

    @pl.loop(0, D // PART)
    def _(n):
        part = hidden[:, pl.ds(pl.multiple_of(n * PART, PART), PART)].astype(F32)
        part = part * part
        for m in range(PART // 128):
            squares[...] += part[:, m * 128:(m + 1) * 128]

    half_copy(1).start()
    mean = jnp.sum(squares[...], axis=1, keepdims=True) * (1.0 / D)
    squares[...] = jnp.broadcast_to(lax.rsqrt(mean + 1e-05), squares.shape)
    q_acc[...] = jnp.zeros_like(q_acc)
    kv_acc[...] = jnp.zeros_like(kv_acc)

    @pl.loop(0, D // PART)
    def _(n):
        cols = pl.ds(pl.multiple_of(n * PART, PART), PART)
        inverse = squares[:, :1]
        normed = (hidden[:, cols].astype(F32) * inverse * gain_ref[:, cols]).astype(BF16)
        q_acc[...] += jnp.dot(normed, wq[cols, :], preferred_element_type=F32)
        kv_acc[...] += lax.dot_general(normed, wkv[:, cols], NT, preferred_element_type=F32)

    queries = q_acc[...].astype(BF16)
    for h in range(2):
        head = queries[:, h * HD:(h + 1) * HD]
        qown[h * SPAN:(h + 1) * SPAN, :] = head[:SPAN]
        qown[PAIR + h * SPAN:PAIR + (h + 1) * SPAN, :] = head[SPAN:2 * SPAN]
        qown[2 * PAIR + h * SAMP:2 * PAIR + (h + 1) * SAMP, :] = head[2 * SPAN:]

    rows_a = pl.ds(pl.multiple_of(x * PAIR, PAIR), PAIR)
    rows_b = pl.ds(pl.multiple_of(GROUP * SPAN + x * PAIR, PAIR), PAIR)
    rows_c = pl.ds(2 * GROUP * SPAN, GROUP * SAMP)
    own_rows = (rows_a, rows_b, pl.ds(pl.multiple_of(2 * GROUP * SPAN + x * 2 * SAMP, 2 * SAMP), 2 * SAMP))
    made_rows = (pl.ds(0, PAIR), pl.ds(PAIR, PAIR), pl.ds(2 * PAIR, 2 * SAMP))

    def q_copy(d, n):
        return remote(
            qown.at[made_rows[n]], qall.at[own_rows[n]], xq_s.at[d * 3 + n], xq_r.at[d * 3 + n], x_peer(d))

    for n in range(3):
        for d in FAR_FIRST:
            q_copy(d, n).start()
        qall[own_rows[n], :] = qown[made_rows[n], :]
    qall[QROWS:, :] = jnp.zeros((QPAD - QROWS, HD), BF16)

    half = kv_acc[...]
    blank = jnp.zeros_like(half)
    piece[...] = jnp.where(
        x % 2 == 0, jnp.concatenate([half, blank], axis=1), jnp.concatenate([blank, half], axis=1)).astype(BF16)

    def piece_copy(d):
        return remote(piece, pieces.at[z], zp_s.at[d], zp_r.at[d], z_peer(d))

    for d in (1, 2, 3):
        piece_copy(d).start()
    pieces[z] = piece[...]

    def wout_columns(to_z, to_x, half):
        return pl.ds(pl.multiple_of((to_z * 4 + to_x) * OUT + half * HALF, HALF), HALF)

    def line_rows(place):
        return pl.ds(pl.multiple_of(place * 256, 256), 256)

    def wout_x_copy(d, n):
        part = 2 * c + n
        return remote(
            wout_hbm.at[:, wout_columns(part, (x + d) % 4, 0)], wout_x.at[part, line_rows(x)],
            xw_s.at[d * 2 + n], xw_r.at[d * 2 + n], x_peer(d))

    def wout_z_copy(d, n):
        part = 2 * c + n
        return remote(
            wout_hbm.at[:, wout_columns((z + d) % 4, part, 1)], wout_z.at[part, line_rows(z)],
            zw_s.at[d * 2 + n], zw_r.at[d * 2 + n], z_peer(d))

    def own_wout_x(n):
        part = 2 * c + n
        return pltpu.make_async_copy(
            wout_hbm.at[:, wout_columns(part, x, 0)], wout_x.at[part, line_rows(x)], wout_load_sem.at[n])

    def own_wout_z(n):
        part = 2 * c + n
        return pltpu.make_async_copy(
            wout_hbm.at[:, wout_columns(z, part, 1)], wout_z.at[part, line_rows(z)], wout_load_sem.at[2 + n])

    def wout_x_share(n):
        part = 2 * c + n
        return remote(wout_x.at[part], wout_x.at[part], xw_s.at[n], xw_r.at[n], (y * 2 + 1 - c, tp))

    def wout_z_share(n):
        part = 2 * c + n
        return remote(wout_z.at[part], wout_z.at[part], zw_s.at[n], zw_r.at[n], (y * 2 + 1 - c, tp))

    acc[...] = jnp.zeros_like(acc)
    stat_m[...] = jnp.full_like(stat_m, -DEAD)
    stat_l[...] = jnp.zeros_like(stat_l)

    def turn_copy(d, kind):
        return remote(
            pieces.at[kind * 2 + z // 2], turn.at[kind, x], xt_s.at[d * 2 + kind], xt_r.at[d * 2 + kind], x_peer(d))

    def numbers_arrived(d):
        slot_copy(d).wait_recv()
        to_smem = pltpu.make_async_copy(slots_in.at[d], slots_smem.at[d], slot_sem.at[d])
        to_smem.start()
        to_smem.wait()

    def arrived(d, k):
        page_copy(d).wait_recv()
        numbers_arrived(d)
        pass_on(k, d)

    for d in (1, 2, 3):
        for n in range(3):
            q_copy(d, n).wait()

    def o_copy(d, part):
        out, into = ((part_out_a, part_in_a), (part_out_b, part_in_b))[part]
        return remote(out.at[d], into.at[d], xo_s.at[d * 2 + part], xo_r.at[d * 2 + part], x_peer(d))

    def l_copy(d, part):
        out, into = ((stat_out_a, stat_in_a), (stat_out_b, stat_in_b))[part]
        return remote(out.at[d], into.at[d], xl_s.at[d * 2 + part], xl_r.at[d * 2 + part], x_peer(d))

    def send_part(part):
        for d in FAR_FIRST:
            start = ((x + d) % 4) * PAIR
            if part == 0:
                cols = pl.ds(pl.multiple_of(start, PAIR), PAIR)
                part_out_a[d, :, :PAIR] = acc[:, cols].astype(BF16)
                part_out_a[d, :, PAIR:] = acc[:, rows_c].astype(BF16)
                stat_out_a[d, 0:1, :PAIR] = stat_m[:, cols]
                stat_out_a[d, 0:1, PAIR:] = stat_m[:, rows_c]
                stat_out_a[d, 1:2, :PAIR] = stat_l[:, cols]
                stat_out_a[d, 1:2, PAIR:] = stat_l[:, rows_c]
            else:
                cols = pl.ds(pl.multiple_of(GROUP * SPAN + start, PAIR), PAIR)
                part_out_b[d] = acc[:, cols].astype(BF16)
                stat_out_b[d, 0:1, :] = stat_m[:, cols]
                stat_out_b[d, 1:2, :] = stat_l[:, cols]
            l_copy(d, part).start()
            o_copy(d, part).start()

    def own_turn():
        for d in (1, 2, 3):
            for kind in range(2):
                turn_copy(d, kind).wait()
        pair = (z % 2) * 2
        turn_keys = turn[0, pair] + turn[0, pair + 1]
        turn_values = turn[1, pair] + turn[1, pair + 1]
        rows = jnp.concatenate([qall[rows_a, :], qall[rows_c, :], qall[rows_b, :]], axis=0)
        count = 2 * PAIR + GROUP * SAMP
        scores = lax.dot_general(turn_keys, rows, NT, preferred_element_type=F32)
        key_idx = lax.broadcasted_iota(jnp.int32, (ROWS, count), 0)
        place = lax.broadcasted_iota(jnp.int32, (ROWS, count), 1)
        token = jnp.where(
            place < PAIR, place % SPAN,
            jnp.where(place < PAIR + GROUP * SAMP, 2 * SPAN + place % SAMP, SPAN + place % SPAN))
        allowed = (key_idx <= token) & ((key_idx < ROWS - SAMP) | (key_idx == token))
        scores = jnp.where(allowed, scores, -DEAD)
        top = jnp.max(scores, axis=0, keepdims=True)
        probs = jnp.exp2(scores * scale - top * scale)
        turn_m[...] = top
        turn_l[...] = jnp.sum(probs, axis=0, keepdims=True)
        turn_o[...] = lax.dot_general(turn_values.T, probs.astype(BF16), NN, preferred_element_type=F32)

    def attend(k, first, chunk, between=None):
        slots = chunk * CAP

        @pl.loop(0, chunk)
        def _(j):
            @pl.when((first + j > 0) & (k != 1))
            def _():
                y_copy(k, first + j).wait_recv()

            @pl.when((first + j > 0) & (k == 1))
            def _():
                half_y_copy(0, first + j).wait_recv()
                half_y_copy(1, first + j).wait_recv()

        live = []
        for j in range(chunk):
            dy, dc = plane_offset(first + j)
            holder = (((y + 4 - dy) % 4) * 2 + (c + dc) % 2) * 16 + ((z + 4 - stage_offset(k)) % 4) * 4 + x
            count = counts_ref[0, holder]
            for slot in range(CAP):
                live.append(count > slot)
        pages = yrecv[k, pl.ds(first, chunk)]
        keys = pages[:, :, :PAGE, :].reshape(slots * PAGE, HD)
        width = pl.ds(0, slots * PAGE)
        vt[:, width] = pages[:, :, PAGE:, :].reshape(slots * PAGE, HD).T

        def some(tiles):
            cols = [pl.ds(t * TILE, TILE) for t in tiles]
            all_scores = [lax.dot_general(keys, qall[own, :], NT, preferred_element_type=F32) for own in cols]
            for own, scores in zip(cols, all_scores):
                old_m = stat_m[:, own]
                new_m = old_m
                for j in range(slots):
                    top = jnp.max(scores[j * PAGE:(j + 1) * PAGE], axis=0, keepdims=True)
                    new_m = jnp.maximum(new_m, jnp.where(live[j], top, -DEAD))
                shift = new_m * scale
                shrink = jnp.exp2(old_m * scale - shift)
                total = stat_l[:, own] * shrink
                weights = []
                for j in range(slots):
                    probs = jnp.exp2(scores[j * PAGE:(j + 1) * PAGE] * scale - jnp.where(live[j], shift, DEAD))
                    total = total + jnp.sum(probs, axis=0, keepdims=True)
                    weights.append(probs.astype(BF16))
                blended = lax.dot_general(
                    vt[:, width], jnp.concatenate(weights, axis=0), NN, preferred_element_type=F32)
                acc[:, own] = acc[:, own] * shrink + blended
                stat_m[:, own] = new_m
                stat_l[:, own] = total

        some(FIRST_TILES)
        if between is not None:
            between()
        some(LATER_TILES)

    def early_step(n, carry):
        attend(n // 2, (n % 2) * EARLY_CHUNK, EARLY_CHUNK)

        @pl.when(n == 0)
        def _():
            numbers_arrived(1)
            half_copy(0).wait_recv()
            pass_half(0)

        @pl.when(n == 1)
        def _():
            half_copy(1).wait_recv()
            pass_half(1)
            arrived(3, 2)
            page_copy(2).start()
            for d in (1, 2, 3):
                piece_copy(d).wait()
            for d in FAR_FIRST:
                for kind in range(2):
                    turn_copy(d, kind).start()
            for kind in range(2):
                turn[kind, x] = pieces[kind * 2 + z // 2]
            for d in FAR_FIRST:
                for m in range(2):
                    wout_x_copy(d, m).start()
            for m in range(2):
                own_wout_x(m).start()
                own_wout_z(m).start()

        @pl.when(n == 2)
        def _():
            own_turn()

        @pl.when(n == 3)
        def _():
            arrived(2, 3)
            for d in FAR_FIRST:
                for m in range(2):
                    wout_z_copy(d, m).start()

        return carry

    def last_step(n, carry):
        def when_last(part):
            @pl.when(n == LAST_STEPS - 1)
            def _():
                send_part(part)

        attend(3, n * LAST_CHUNK, LAST_CHUNK, lambda: when_last(0))
        when_last(1)

        @pl.when(n == 0)
        def _():
            for m in range(2):
                for d in (1, 2, 3):
                    wout_x_copy(d, m).wait()
                own_wout_x(m).wait()
                wout_x_share(m).start()

        @pl.when(n == 1)
        def _():
            for m in range(2):
                for d in (1, 2, 3):
                    wout_z_copy(d, m).wait()
                own_wout_z(m).wait()
                wout_z_share(m).start()

        return carry

    lax.fori_loop(0, EARLY_STEPS, early_step, 0)
    lax.fori_loop(0, LAST_STEPS, last_step, 0)

    def merge(own, part, turn_cols):
        into, stats = ((part_in_a, stat_in_a), (part_in_b, stat_in_b))[part]
        for d in (1, 2, 3):
            l_copy(d, part).wait()
            o_copy(d, part).wait()
        tops = [jnp.concatenate([stat_m[:, cols] for cols in own], axis=1) * scale, turn_m[:, turn_cols] * scale]
        sums = [jnp.concatenate([stat_l[:, cols] for cols in own], axis=1), turn_l[:, turn_cols]]
        sources = [jnp.concatenate([acc[:, cols] for cols in own], axis=1), turn_o[:, turn_cols]]
        for d in (1, 2, 3):
            tops.append(stats[d, 0:1, :] * scale)
            sums.append(stats[d, 1:2, :])
            sources.append(into[d].astype(F32))
        top = tops[0]
        for other in tops[1:]:
            top = jnp.maximum(top, other)
        shares = [jnp.exp2(one - top) for one in tops]
        norm = sums[0] * shares[0]
        for one, share in zip(sums[1:], shares[1:]):
            norm = norm + one * share
        inverse = 1.0 / norm
        merged = sources[0] * (shares[0] * inverse)
        for one, share in zip(sources[1:], shares[1:]):
            merged = merged + one * (share * inverse)
        return merged

    def ax_copy(d, part):
        out, into = ((att_out_a, att_xa), (att_out_b, att_xb))[part]
        return remote(
            out.at[pl.ds(0, PAIR)], into.at[rows_a], xa_s.at[d * 2 + part], xa_r.at[d * 2 + part], x_peer(d))

    def az_copy(d, part):
        out, into = ((att_out_a, att_za), (att_out_b, att_zb))[part]
        return remote(out, into.at[z], za_s.at[d * 2 + part], za_r.at[d * 2 + part], z_peer(d))

    merged = merge([rows_a, rows_c], 0, pl.ds(0, PAIR + GROUP * SAMP)).T.astype(BF16)
    samples[...] = merged[PAIR:]
    att_out_a[:PAIR, :] = merged[:PAIR]
    att_out_a[PAIR:, :] = samples[pl.ds(pl.multiple_of(x * 2 * SAMP, 2 * SAMP), 2 * SAMP), :]
    for d in FAR_FIRST:
        ax_copy(d, 0).start()
        az_copy(d, 0).start()
    att_xa[rows_a, :] = att_out_a[:PAIR, :]
    att_za[z] = att_out_a[...]
    att_out_b[...] = merge([rows_b], 1, pl.ds(PAIR + GROUP * SAMP, PAIR)).T.astype(BF16)
    for d in FAR_FIRST:
        ax_copy(d, 1).start()
        az_copy(d, 1).start()
    att_xb[rows_a, :] = att_out_b[...]
    att_zb[z] = att_out_b[...]

    def sum_z_copy(d, part):
        out, into = ((sum_out_za, sum_in_za), (sum_out_zb, sum_in_zb))[part]
        return remote(out.at[d], into.at[d], zo_s.at[d * 2 + part], zo_r.at[d * 2 + part], z_peer(d))

    def sum_x_copy(d, part):
        out, into = ((sum_out_xa, sum_in_xa), (sum_out_xb, sum_in_xb))[part]
        return remote(out.at[d], into.at[d], xo2_s.at[d * 2 + part], xo2_r.at[d * 2 + part], x_peer(d))

    def project(part, attended_x, attended_z):
        out_x, out_z = ((sum_out_xa, sum_out_za), (sum_out_xb, sum_out_zb))[part]
        for d in FAR_FIRST:
            out_z[d] = jnp.dot(attended_x, wout_x[(z + d) % 4], preferred_element_type=F32).astype(BF16)
            sum_z_copy(d, part).start()
            out_x[d] = jnp.dot(attended_z, wout_z[(x + d) % 4], preferred_element_type=F32).astype(BF16)
            sum_x_copy(d, part).start()

    def line_up(ref, start, size):
        return jnp.concatenate(
            [ref[m, start + h * size:start + (h + 1) * size, :] for m in range(4) for h in range(2)], axis=1)

    for m in range(2):
        wout_x_share(m).wait()
        wout_z_share(m).wait()
    for d in (1, 2, 3):
        ax_copy(d, 0).wait()
        az_copy(d, 0).wait()
    early_x = jnp.concatenate(
        [
            jnp.concatenate([att_xa[h * SPAN:(h + 1) * SPAN, :] for h in range(GROUP)], axis=1),
            jnp.concatenate([samples[h * SAMP:(h + 1) * SAMP, :] for h in range(GROUP)], axis=1),
        ],
        axis=0)
    early_z = jnp.concatenate([line_up(att_za, 0, SPAN), line_up(att_za, PAIR, SAMP)], axis=0)
    project(0, early_x, early_z)
    for d in (1, 2, 3):
        ax_copy(d, 1).wait()
        az_copy(d, 1).wait()
    late_x = jnp.concatenate([att_xb[h * SPAN:(h + 1) * SPAN, :] for h in range(GROUP)], axis=1)
    late_z = line_up(att_zb, 0, SPAN)
    project(1, late_x, late_z)
    sums_z = [jnp.dot(one, wout_x[z], preferred_element_type=F32) for one in (early_x, late_x)]
    sums_x = [jnp.dot(one, wout_z[x], preferred_element_type=F32) for one in (early_z, late_z)]
    for part in range(2):
        sum_x, sum_z = sums_x[part], sums_z[part]
        in_x, in_z = ((sum_in_xa, sum_in_za), (sum_in_xb, sum_in_zb))[part]
        for d in (1, 2, 3):
            sum_z_copy(d, part).wait()
            sum_z = sum_z + in_z[d].astype(F32)
            sum_x_copy(d, part).wait()
            sum_x = sum_x + in_x[d].astype(F32)
        for total, cols in ((sum_z, slice(0, HALF)), (sum_x, slice(HALF, OUT))):
            if part == 0:
                out_ref[:SPAN, cols] = total[:SPAN].astype(BF16)
                out_ref[2 * SPAN:, cols] = total[SPAN:].astype(BF16)
            else:
                out_ref[SPAN:2 * SPAN, cols] = total.astype(BF16)

    for d in (1, 2, 3):
        slot_copy(d).wait_send()
    for d in (2, 3):
        page_copy(d).wait_send()
    for half in range(2):
        half_copy(half).wait_send()

    @pl.loop(0, 4)
    def _(k):
        @pl.loop(1, SOURCES)
        def _(i):
            @pl.when(k != 1)
            def _():
                y_copy(k, i).wait_send()

            @pl.when(k == 1)
            def _():
                half_y_copy(0, i).wait_send()
                half_y_copy(1, i).wait_send()


def local(hidden_in, norm_gain, w_query, w_keyval, w_out, kv_store, page_slots, page_counts):
    vmem = pl.BlockSpec(memory_space=pltpu.VMEM)
    anywhere = pl.BlockSpec(memory_space=pl.ANY)
    dma = pltpu.SemaphoreType.DMA
    slots = page_slots.transpose(2, 1, 0)
    return pl.pallas_call(
        layer_kernel,
        out_shape=pltpu.VMEM((ROWS, OUT), BF16),
        in_specs=[anywhere, anywhere, anywhere, anywhere, anywhere, anywhere, anywhere, anywhere],
        out_specs=vmem,
        scratch_shapes=[
            pltpu.SMEM((1, 128), jnp.int32),
            pltpu.VMEM((1, D), F32),
            pltpu.VMEM((CAP, 1, 8), jnp.int32),
            pltpu.VMEM((ROWS, D), BF16),
            pltpu.VMEM((D, 256), BF16),
            pltpu.VMEM((64, D), BF16),
            pltpu.VMEM((4, 1024, HALF), BF16),
            pltpu.VMEM((4, 1024, HALF), BF16),
            pltpu.VMEM((16, 2 * PAGE, HD), BF16),
            pltpu.VMEM((16, PAGE, HD), BF16),
            pltpu.VMEM((16, PAGE, HD), BF16),
            pltpu.VMEM((16, 2 * PAGE, HD), BF16),
            pltpu.VMEM((16, 2 * PAGE, HD), BF16),
            pltpu.VMEM((8, 128), jnp.int32),
            pltpu.VMEM((4, 8, 128), jnp.int32),
            pltpu.SMEM((4, 8, 128), jnp.int32),
            pltpu.VMEM((4, SOURCES, CAP, 2 * PAGE, HD), BF16),
            pltpu.VMEM((4, SOURCES, CAP, 2 * PAGE, HD), BF16),
            pltpu.VMEM((ROWS, 128), F32),
            pltpu.VMEM((ROWS, 256), F32),
            pltpu.VMEM((ROWS, 64), F32),
            pltpu.VMEM((2 * ROWS, HD), BF16),
            pltpu.VMEM((QPAD, HD), BF16),
            pltpu.VMEM((ROWS, HD), BF16),
            pltpu.VMEM((4, ROWS, HD), BF16),
            pltpu.VMEM((2, 4, ROWS, HD), BF16),
            pltpu.VMEM((HD, QPAD), F32),
            pltpu.VMEM((1, QPAD), F32),
            pltpu.VMEM((1, QPAD), F32),
            pltpu.VMEM((HD, EARLY_CHUNK * CAP * PAGE), BF16),
            pltpu.VMEM((HD, 2 * PAIR + 128), F32),
            pltpu.VMEM((1, 2 * PAIR + 128), F32),
            pltpu.VMEM((1, 2 * PAIR + 128), F32),
            pltpu.VMEM((4, HD, PAIR + 128), BF16),
            pltpu.VMEM((4, HD, PAIR + 128), BF16),
            pltpu.VMEM((4, 2, PAIR + 128), F32),
            pltpu.VMEM((4, 2, PAIR + 128), F32),
            pltpu.VMEM((4, HD, PAIR), BF16),
            pltpu.VMEM((4, HD, PAIR), BF16),
            pltpu.VMEM((4, 2, PAIR), F32),
            pltpu.VMEM((4, 2, PAIR), F32),
            pltpu.VMEM((PAIR + 2 * SAMP, HD), BF16),
            pltpu.VMEM((PAIR, HD), BF16),
            pltpu.VMEM((GROUP * SAMP, HD), BF16),
            pltpu.VMEM((4 * PAIR, HD), BF16),
            pltpu.VMEM((4 * PAIR, HD), BF16),
            pltpu.VMEM((4, PAIR + 2 * SAMP, HD), BF16),
            pltpu.VMEM((4, PAIR, HD), BF16),
            pltpu.VMEM((4, EARLY, HALF), BF16),
            pltpu.VMEM((4, EARLY, HALF), BF16),
            pltpu.VMEM((4, SPAN, HALF), BF16),
            pltpu.VMEM((4, SPAN, HALF), BF16),
            pltpu.VMEM((4, EARLY, HALF), BF16),
            pltpu.VMEM((4, EARLY, HALF), BF16),
            pltpu.VMEM((4, SPAN, HALF), BF16),
            pltpu.VMEM((4, SPAN, HALF), BF16),
            dma((7,)), dma((4,)), dma((4,)),
            dma((4,)), dma((4,)), dma((4,)), dma((4,)), dma((4,)), dma((4,)),
            dma((5 * SOURCES,)), dma((5 * SOURCES,)),
            dma((12,)), dma((12,)), dma((8,)), dma((8,)), dma((8,)), dma((8,)),
            dma((8,)), dma((8,)),
            dma((8,)), dma((8,)), dma((8,)), dma((8,)), dma((8,)), dma((8,)),
            dma((8,)), dma((8,)), dma((8,)), dma((8,)), dma((8,)), dma((8,)),
        ],
        compiler_params=pltpu.CompilerParams(
            collective_id=1, has_side_effects=True, vmem_limit_bytes=62 * 2**20),
        cost_estimate=pl.CostEstimate(flops=17 * 10**9, bytes_accessed=19 * 10**6, transcendentals=27 * 10**6),
        name="layer",
    )(
        slots, page_counts, norm_gain.reshape(1, D), hidden_in, w_query, w_keyval.T, w_out,
        kv_store.reshape(16, 4, 2 * PAGE, HD))


def solution(mesh):
    return jax.shard_map(
        local,
        mesh=mesh,
        in_specs=(
            P("pool", None),
            P(),
            P(None, "tp"),
            P(None, "tp"),
            P("tp", None),
            P(("pool", "tp"), None, None, None, None),
            P(None, ("pool", "tp"), None),
            P("pool", None),
        ),
        out_specs=P("pool", "tp"),
        check_vma=False,
    )
```

```python
import math

import jax
import jax.numpy as jnp
from jax import lax
from jax.experimental import pallas as pl
from jax.experimental.pallas import tpu as pltpu
from jax.sharding import PartitionSpec as P

SAMP = 16
MESH = pl.DeviceIdType.MESH
F32 = jnp.float32
BF16 = jnp.bfloat16
PAGE = 128
HD = 128
CAP = 3
D = 8192
LOG2E = 1.4426950408889634
DEAD = 1e30
ROWS = 272
GROUP = 8
SPAN = 128
PAIR = 2 * SPAN
EARLY = 144
QROWS = GROUP * ROWS
QPAD = 2304
TILE = 256
FIRST_TILES = (0, 1, 2, 3, 8)
LATER_TILES = (4, 5, 6, 7)
SOURCES = 8
EARLY_CHUNK = 4
LAST_CHUNK = 2
EARLY_STEPS = 7
LAST_STEPS = 2
HALF = 256
PART = 512
OUT = 512
NT = (((1,), (1,)), ((), ()))
NN = (((1,), (0,)), ((), ()))
FAR_FIRST = (2, 1, 3)


def plane_offset(i):
    dy = jnp.where(i < 2, 0, jnp.where(i < 6, 1 + 2 * (i % 2), 2))
    dc = jnp.where((i >= 2) & (i < 6), (i - 2) // 2, i % 2)
    return dy, dc


def stage_offset(k):
    return jnp.where(k < 2, k, 5 - k)


def layer_kernel(
    slots_hbm, counts_hbm, gain_hbm, hidden_hbm, wq_hbm, wkv_hbm, wout_hbm, kv_hbm, out_ref,
    counts_ref, gain_ref, slots_own, hidden, wq, wkv, wout_x, wout_z, held0, keys1, values1, held2, held3, slots_out, slots_in, slots_smem,
    ysend, yrecv, squares, q_acc, kv_acc, qown, qall, piece, pieces, turn,
    acc, stat_m, stat_l, vt, turn_o, turn_m, turn_l,
    part_out_a, part_in_a, stat_out_a, stat_in_a, part_out_b, part_in_b, stat_out_b, stat_in_b,
    att_out_a, att_out_b, samples, att_xa, att_xb, att_za, att_zb,
    sum_out_xa, sum_in_xa, sum_out_xb, sum_in_xb, sum_out_za, sum_in_za, sum_out_zb, sum_in_zb,
    load_sem, wout_load_sem, slot_sem, zk_s, zk_r, zs_s, zs_r, zp_s, zp_r, y_s, y_r,
    xq_s, xq_r, xt_s, xt_r, xw_s, xw_r, zw_s, zw_r,
    xo_s, xo_r, xl_s, xl_r, xa_s, xa_r, za_s, za_r, xo2_s, xo2_r, zo_s, zo_r,
):
    pool = lax.axis_index("pool")
    tp = lax.axis_index("tp")
    y, c = pool // 2, pool % 2
    z, x = tp // 4, tp % 4
    scale = LOG2E / math.sqrt(HD)
    held = (held0, None, held2, held3)

    def x_peer(d):
        return (pool, z * 4 + (x + d) % 4)

    def z_peer(d):
        return (pool, ((z + d) % 4) * 4 + x)

    def plane_peer(i):
        dy, dc = plane_offset(i)
        return ((y + dy) % 4) * 2 + (c + dc) % 2

    def remote(src, dst, send_sem, recv_sem, device):
        return pltpu.make_async_remote_copy(
            src_ref=src, dst_ref=dst, send_sem=send_sem, recv_sem=recv_sem, device_id=device, device_id_type=MESH)

    own_pages = pltpu.make_async_copy(kv_hbm.at[:, z], held0, load_sem.at[0])
    own_pages.start()
    fetch_slots = pltpu.make_async_copy(slots_hbm, slots_own, load_sem.at[4])
    fetch_slots.start()
    loads = [
        pltpu.make_async_copy(hidden_hbm, hidden, load_sem.at[1]),
        pltpu.make_async_copy(wq_hbm, wq, load_sem.at[2]),
        pltpu.make_async_copy(wkv_hbm, wkv, load_sem.at[3]),
        pltpu.make_async_copy(gain_hbm, gain_ref, load_sem.at[5]),
        pltpu.make_async_copy(counts_hbm, counts_ref, load_sem.at[6]),
    ]
    barrier = pltpu.get_barrier_semaphore()
    for i in range(1, SOURCES):
        pl.semaphore_signal(barrier, inc=1, device_id=(plane_peer(i), tp), device_id_type=MESH)
    for d in (1, 2, 3):
        pl.semaphore_signal(barrier, inc=1, device_id=x_peer(d), device_id_type=MESH)
        pl.semaphore_signal(barrier, inc=1, device_id=z_peer(d), device_id_type=MESH)

    for load in loads:
        load.start()
    fetch_slots.wait()
    for slot in range(CAP):
        slots_out[slot:slot + 1, :8] = slots_own[slot]
    own_slots = pltpu.make_async_copy(slots_out, slots_smem.at[0], slot_sem.at[0])
    own_slots.start()
    pl.semaphore_wait(barrier, SOURCES - 1 + 6)

    def slot_copy(d):
        return remote(slots_out, slots_in.at[d], zs_s.at[d], zs_r.at[d], z_peer(d))

    def page_copy(d):
        return remote(kv_hbm.at[:, (z + d) % 4], held[d], zk_s.at[d], zk_r.at[d], z_peer(d))

    def half_copy(half):
        into = (keys1, values1)[half]
        source = kv_hbm.at[:, (z + 1) % 4, pl.ds(half * PAGE, PAGE)]
        return remote(source, into, zk_s.at[half], zk_r.at[half], z_peer(1))

    for d in (1, 3, 2):
        slot_copy(d).start()
    half_copy(0).start()
    page_copy(3).start()

    def y_copy(k, i):
        return remote(
            ysend.at[k, i], yrecv.at[k, i], y_s.at[k * SOURCES + i], y_r.at[k * SOURCES + i], (plane_peer(i), tp))

    def half_y_copy(half, i):
        rows = pl.ds(half * PAGE, PAGE)
        own = (1 + 3 * half) * SOURCES + i
        return remote(
            ysend.at[1, i, :, rows], yrecv.at[1, i, :, rows], y_s.at[own], y_r.at[own], (plane_peer(i), tp))

    def pass_on(k, d):
        for slot in range(CAP):
            yrecv[k, 0, slot] = held[d][slots_smem[d, slot, pool]]

        @pl.loop(1, SOURCES)
        def _(i):
            dest = plane_peer(i)
            for slot in range(CAP):
                ysend[k, i, slot] = held[d][slots_smem[d, slot, dest]]
            y_copy(k, i).start()

    def pass_half(half):
        pages = (keys1, values1)[half]
        rows = pl.ds(half * PAGE, PAGE)
        for slot in range(CAP):
            yrecv[1, 0, slot, rows] = pages[slots_smem[1, slot, pool]]

        @pl.loop(1, SOURCES)
        def _(i):
            dest = plane_peer(i)
            for slot in range(CAP):
                ysend[1, i, slot, rows] = pages[slots_smem[1, slot, dest]]
            half_y_copy(half, i).start()

    own_slots.wait()
    own_pages.wait()
    pass_on(0, 0)

    for load in loads:
        load.wait()
    squares[...] = jnp.zeros_like(squares)

    @pl.loop(0, D // PART)
    def _(n):
        part = hidden[:, pl.ds(pl.multiple_of(n * PART, PART), PART)].astype(F32)
        part = part * part
        for m in range(PART // 128):
            squares[...] += part[:, m * 128:(m + 1) * 128]

    half_copy(1).start()
    mean = jnp.sum(squares[...], axis=1, keepdims=True) * (1.0 / D)
    squares[...] = jnp.broadcast_to(lax.rsqrt(mean + 1e-05), squares.shape)
    q_acc[...] = jnp.zeros_like(q_acc)
    kv_acc[...] = jnp.zeros_like(kv_acc)

    @pl.loop(0, D // PART)
    def _(n):
        cols = pl.ds(pl.multiple_of(n * PART, PART), PART)
        inverse = squares[:, :1]
        normed = (hidden[:, cols].astype(F32) * inverse * gain_ref[:, cols]).astype(BF16)
        q_acc[...] += jnp.dot(normed, wq[cols, :], preferred_element_type=F32)
        kv_acc[...] += lax.dot_general(normed, wkv[:, cols], NT, preferred_element_type=F32)

    queries = q_acc[...].astype(BF16)
    for h in range(2):
        head = queries[:, h * HD:(h + 1) * HD]
        qown[h * SPAN:(h + 1) * SPAN, :] = head[:SPAN]
        qown[PAIR + h * SPAN:PAIR + (h + 1) * SPAN, :] = head[SPAN:2 * SPAN]
        qown[2 * PAIR + h * SAMP:2 * PAIR + (h + 1) * SAMP, :] = head[2 * SPAN:]

    rows_a = pl.ds(pl.multiple_of(x * PAIR, PAIR), PAIR)
    rows_b = pl.ds(pl.multiple_of(GROUP * SPAN + x * PAIR, PAIR), PAIR)
    rows_c = pl.ds(2 * GROUP * SPAN, GROUP * SAMP)
    own_rows = (rows_a, rows_b, pl.ds(pl.multiple_of(2 * GROUP * SPAN + x * 2 * SAMP, 2 * SAMP), 2 * SAMP))
    made_rows = (pl.ds(0, PAIR), pl.ds(PAIR, PAIR), pl.ds(2 * PAIR, 2 * SAMP))

    def q_copy(d, n):
        return remote(
            qown.at[made_rows[n]], qall.at[own_rows[n]], xq_s.at[d * 3 + n], xq_r.at[d * 3 + n], x_peer(d))

    for n in range(3):
        for d in FAR_FIRST:
            q_copy(d, n).start()
        qall[own_rows[n], :] = qown[made_rows[n], :]
    qall[QROWS:, :] = jnp.zeros((QPAD - QROWS, HD), BF16)

    half = kv_acc[...]
    blank = jnp.zeros_like(half)
    piece[...] = jnp.where(
        x % 2 == 0, jnp.concatenate([half, blank], axis=1), jnp.concatenate([blank, half], axis=1)).astype(BF16)

    def piece_copy(d):
        return remote(piece, pieces.at[z], zp_s.at[d], zp_r.at[d], z_peer(d))

    for d in (1, 2, 3):
        piece_copy(d).start()
    pieces[z] = piece[...]

    def wout_columns(to_z, to_x, half):
        return pl.ds(pl.multiple_of((to_z * 4 + to_x) * OUT + half * HALF, HALF), HALF)

    def line_rows(place):
        return pl.ds(pl.multiple_of(place * 256, 256), 256)

    def wout_x_copy(d, n):
        part = 2 * c + n
        return remote(
            wout_hbm.at[:, wout_columns(part, (x + d) % 4, 0)], wout_x.at[part, line_rows(x)],
            xw_s.at[d * 2 + n], xw_r.at[d * 2 + n], x_peer(d))

    def wout_z_copy(d, n):
        part = 2 * c + n
        return remote(
            wout_hbm.at[:, wout_columns((z + d) % 4, part, 1)], wout_z.at[part, line_rows(z)],
            zw_s.at[d * 2 + n], zw_r.at[d * 2 + n], z_peer(d))

    def own_wout_x(n):
        part = 2 * c + n
        return pltpu.make_async_copy(
            wout_hbm.at[:, wout_columns(part, x, 0)], wout_x.at[part, line_rows(x)], wout_load_sem.at[n])

    def own_wout_z(n):
        part = 2 * c + n
        return pltpu.make_async_copy(
            wout_hbm.at[:, wout_columns(z, part, 1)], wout_z.at[part, line_rows(z)], wout_load_sem.at[2 + n])

    def wout_x_share(n):
        part = 2 * c + n
        return remote(wout_x.at[part], wout_x.at[part], xw_s.at[n], xw_r.at[n], (y * 2 + 1 - c, tp))

    def wout_z_share(n):
        part = 2 * c + n
        return remote(wout_z.at[part], wout_z.at[part], zw_s.at[n], zw_r.at[n], (y * 2 + 1 - c, tp))

    acc[...] = jnp.zeros_like(acc)
    vt[HD:, :] = jnp.ones_like(vt[HD:, :])
    stat_m[...] = jnp.full_like(stat_m, -DEAD)
    stat_l[...] = jnp.zeros_like(stat_l)

    def turn_copy(d, kind):
        return remote(
            pieces.at[kind * 2 + z // 2], turn.at[kind, x], xt_s.at[d * 2 + kind], xt_r.at[d * 2 + kind], x_peer(d))

    def numbers_arrived(d):
        slot_copy(d).wait_recv()
        to_smem = pltpu.make_async_copy(slots_in.at[d], slots_smem.at[d], slot_sem.at[d])
        to_smem.start()
        to_smem.wait()

    def arrived(d, k):
        page_copy(d).wait_recv()
        numbers_arrived(d)
        pass_on(k, d)

    for d in (1, 2, 3):
        for n in range(3):
            q_copy(d, n).wait()

    def o_copy(d, part):
        out, into = ((part_out_a, part_in_a), (part_out_b, part_in_b))[part]
        return remote(out.at[d], into.at[d], xo_s.at[d * 2 + part], xo_r.at[d * 2 + part], x_peer(d))

    def l_copy(d, part):
        out, into = ((stat_out_a, stat_in_a), (stat_out_b, stat_in_b))[part]
        return remote(out.at[d], into.at[d], xl_s.at[d * 2 + part], xl_r.at[d * 2 + part], x_peer(d))

    def send_part(part):
        for d in FAR_FIRST:
            start = ((x + d) % 4) * PAIR
            if part == 0:
                cols = pl.ds(pl.multiple_of(start, PAIR), PAIR)
                part_out_a[d, :, :PAIR] = acc[:, cols].astype(BF16)
                part_out_a[d, :, PAIR:] = acc[:, rows_c].astype(BF16)
                stat_out_a[d, 0:1, :PAIR] = stat_m[:, cols]
                stat_out_a[d, 0:1, PAIR:] = stat_m[:, rows_c]
                stat_out_a[d, 1:2, :PAIR] = stat_l[:, cols]
                stat_out_a[d, 1:2, PAIR:] = stat_l[:, rows_c]
            else:
                cols = pl.ds(pl.multiple_of(GROUP * SPAN + start, PAIR), PAIR)
                part_out_b[d] = acc[:, cols].astype(BF16)
                stat_out_b[d, 0:1, :] = stat_m[:, cols]
                stat_out_b[d, 1:2, :] = stat_l[:, cols]
            l_copy(d, part).start()
            o_copy(d, part).start()

    def own_turn():
        for d in (1, 2, 3):
            for kind in range(2):
                turn_copy(d, kind).wait()
        pair = (z % 2) * 2
        turn_keys = turn[0, pair] + turn[0, pair + 1]
        turn_values = turn[1, pair] + turn[1, pair + 1]
        rows = jnp.concatenate([qall[rows_a, :], qall[rows_c, :], qall[rows_b, :]], axis=0)
        count = 2 * PAIR + GROUP * SAMP
        scores = lax.dot_general(turn_keys, rows, NT, preferred_element_type=F32)
        key_idx = lax.broadcasted_iota(jnp.int32, (ROWS, count), 0)
        place = lax.broadcasted_iota(jnp.int32, (ROWS, count), 1)
        token = jnp.where(
            place < PAIR, place % SPAN,
            jnp.where(place < PAIR + GROUP * SAMP, 2 * SPAN + place % SAMP, SPAN + place % SPAN))
        allowed = (key_idx <= token) & ((key_idx < ROWS - SAMP) | (key_idx == token))
        scores = jnp.where(allowed, scores, -DEAD)
        top = jnp.max(scores, axis=0, keepdims=True)
        probs = jnp.exp2(scores * scale - top * scale)
        turn_m[...] = top
        turn_l[...] = jnp.sum(probs, axis=0, keepdims=True)
        turn_o[...] = lax.dot_general(turn_values.T, probs.astype(BF16), NN, preferred_element_type=F32)

    def attend(k, first, chunk, between=None):
        slots = chunk * CAP

        @pl.loop(0, chunk)
        def _(j):
            @pl.when((first + j > 0) & (k != 1))
            def _():
                y_copy(k, first + j).wait_recv()

            @pl.when((first + j > 0) & (k == 1))
            def _():
                half_y_copy(0, first + j).wait_recv()
                half_y_copy(1, first + j).wait_recv()

        live = []
        for j in range(chunk):
            dy, dc = plane_offset(first + j)
            holder = (((y + 4 - dy) % 4) * 2 + (c + dc) % 2) * 16 + ((z + 4 - stage_offset(k)) % 4) * 4 + x
            count = counts_ref[0, holder]
            for slot in range(CAP):
                live.append(count > slot)
        pages = yrecv[k, pl.ds(first, chunk)]
        keys = pages[:, :, :PAGE, :].reshape(slots * PAGE, HD)
        width = pl.ds(0, slots * PAGE)
        vt[:HD, width] = pages[:, :, PAGE:, :].reshape(slots * PAGE, HD).T

        def some(tiles):
            cols = [pl.ds(t * TILE, TILE) for t in tiles]
            all_scores = [lax.dot_general(keys, qall[own, :], NT, preferred_element_type=F32) for own in cols]
            for own, scores in zip(cols, all_scores):
                old_m = stat_m[:, own]
                new_m = old_m
                for j in range(slots):
                    top = jnp.max(scores[j * PAGE:(j + 1) * PAGE], axis=0, keepdims=True)
                    new_m = jnp.maximum(new_m, jnp.where(live[j], top, -DEAD))
                shift = new_m * scale
                shrink = jnp.exp2(old_m * scale - shift)
                weights = []
                for j in range(slots):
                    probs = jnp.exp2(scores[j * PAGE:(j + 1) * PAGE] * scale - jnp.where(live[j], shift, DEAD))
                    weights.append(probs.astype(BF16))
                blended = lax.dot_general(
                    vt[:, width], jnp.concatenate(weights, axis=0), NN, preferred_element_type=F32)
                acc[:, own] = acc[:, own] * shrink + blended[:HD]
                stat_m[:, own] = new_m
                stat_l[:, own] = stat_l[:, own] * shrink + blended[HD:HD + 1]

        some(FIRST_TILES)
        if between is not None:
            between()
        some(LATER_TILES)

    def early_step(n, carry):
        attend(n // 2, (n % 2) * EARLY_CHUNK, EARLY_CHUNK)

        @pl.when(n == 0)
        def _():
            numbers_arrived(1)
            half_copy(0).wait_recv()
            pass_half(0)

        @pl.when(n == 1)
        def _():
            half_copy(1).wait_recv()
            pass_half(1)
            arrived(3, 2)
            page_copy(2).start()
            for d in (1, 2, 3):
                piece_copy(d).wait()
            for d in FAR_FIRST:
                for kind in range(2):
                    turn_copy(d, kind).start()
            for kind in range(2):
                turn[kind, x] = pieces[kind * 2 + z // 2]
            for d in FAR_FIRST:
                for m in range(2):
                    wout_x_copy(d, m).start()
            for m in range(2):
                own_wout_x(m).start()
                own_wout_z(m).start()

        @pl.when(n == 2)
        def _():
            own_turn()

        @pl.when(n == 3)
        def _():
            arrived(2, 3)
            for d in FAR_FIRST:
                for m in range(2):
                    wout_z_copy(d, m).start()

        @pl.when(n == 5)
        def _():
            for m in range(2):
                for d in (1, 2, 3):
                    wout_x_copy(d, m).wait()
                own_wout_x(m).wait()
                wout_x_share(m).start()

        @pl.when(n == 6)
        def _():
            for m in range(2):
                for d in (1, 2, 3):
                    wout_z_copy(d, m).wait()
                own_wout_z(m).wait()
                wout_z_share(m).start()

        return carry

    def last_step(n, carry):
        def when_last(part):
            @pl.when(n == LAST_STEPS - 1)
            def _():
                send_part(part)

        attend(3, EARLY_CHUNK + n * LAST_CHUNK, LAST_CHUNK, lambda: when_last(0))
        when_last(1)

        return carry

    lax.fori_loop(0, EARLY_STEPS, early_step, 0)
    lax.fori_loop(0, LAST_STEPS, last_step, 0)

    def merge(own, part, turn_cols):
        into, stats = ((part_in_a, stat_in_a), (part_in_b, stat_in_b))[part]
        for d in (1, 2, 3):
            l_copy(d, part).wait()
            o_copy(d, part).wait()
        tops = [jnp.concatenate([stat_m[:, cols] for cols in own], axis=1) * scale, turn_m[:, turn_cols] * scale]
        sums = [jnp.concatenate([stat_l[:, cols] for cols in own], axis=1), turn_l[:, turn_cols]]
        sources = [jnp.concatenate([acc[:, cols] for cols in own], axis=1), turn_o[:, turn_cols]]
        for d in (1, 2, 3):
            tops.append(stats[d, 0:1, :] * scale)
            sums.append(stats[d, 1:2, :])
            sources.append(into[d].astype(F32))
        top = tops[0]
        for other in tops[1:]:
            top = jnp.maximum(top, other)
        shares = [jnp.exp2(one - top) for one in tops]
        norm = sums[0] * shares[0]
        for one, share in zip(sums[1:], shares[1:]):
            norm = norm + one * share
        inverse = 1.0 / norm
        merged = sources[0] * (shares[0] * inverse)
        for one, share in zip(sources[1:], shares[1:]):
            merged = merged + one * (share * inverse)
        return merged

    def ax_copy(d, part):
        out, into = ((att_out_a, att_xa), (att_out_b, att_xb))[part]
        return remote(
            out.at[pl.ds(0, PAIR)], into.at[rows_a], xa_s.at[d * 2 + part], xa_r.at[d * 2 + part], x_peer(d))

    def az_copy(d, part):
        out, into = ((att_out_a, att_za), (att_out_b, att_zb))[part]
        return remote(out, into.at[z], za_s.at[d * 2 + part], za_r.at[d * 2 + part], z_peer(d))

    merged = merge([rows_a, rows_c], 0, pl.ds(0, PAIR + GROUP * SAMP)).T.astype(BF16)
    samples[...] = merged[PAIR:]
    att_out_a[:PAIR, :] = merged[:PAIR]
    att_out_a[PAIR:, :] = samples[pl.ds(pl.multiple_of(x * 2 * SAMP, 2 * SAMP), 2 * SAMP), :]
    for d in FAR_FIRST:
        ax_copy(d, 0).start()
        az_copy(d, 0).start()
    att_xa[rows_a, :] = att_out_a[:PAIR, :]
    att_za[z] = att_out_a[...]
    att_out_b[...] = merge([rows_b], 1, pl.ds(PAIR + GROUP * SAMP, PAIR)).T.astype(BF16)
    for d in FAR_FIRST:
        ax_copy(d, 1).start()
        az_copy(d, 1).start()
    att_xb[rows_a, :] = att_out_b[...]
    att_zb[z] = att_out_b[...]

    def sum_z_copy(d, part):
        out, into = ((sum_out_za, sum_in_za), (sum_out_zb, sum_in_zb))[part]
        return remote(out.at[d], into.at[d], zo_s.at[d * 2 + part], zo_r.at[d * 2 + part], z_peer(d))

    def sum_x_copy(d, part):
        out, into = ((sum_out_xa, sum_in_xa), (sum_out_xb, sum_in_xb))[part]
        return remote(out.at[d], into.at[d], xo2_s.at[d * 2 + part], xo2_r.at[d * 2 + part], x_peer(d))

    def project(part, attended_x, attended_z):
        out_x, out_z = ((sum_out_xa, sum_out_za), (sum_out_xb, sum_out_zb))[part]
        for d in FAR_FIRST:
            out_z[d] = jnp.dot(attended_x, wout_x[(z + d) % 4], preferred_element_type=F32).astype(BF16)
            sum_z_copy(d, part).start()
            out_x[d] = jnp.dot(attended_z, wout_z[(x + d) % 4], preferred_element_type=F32).astype(BF16)
            sum_x_copy(d, part).start()

    def line_up(ref, start, size):
        return jnp.concatenate(
            [ref[m, start + h * size:start + (h + 1) * size, :] for m in range(4) for h in range(2)], axis=1)

    for m in range(2):
        wout_x_share(m).wait()
        wout_z_share(m).wait()
    for d in (1, 2, 3):
        ax_copy(d, 0).wait()
        az_copy(d, 0).wait()
    early_x = jnp.concatenate(
        [
            jnp.concatenate([att_xa[h * SPAN:(h + 1) * SPAN, :] for h in range(GROUP)], axis=1),
            jnp.concatenate([samples[h * SAMP:(h + 1) * SAMP, :] for h in range(GROUP)], axis=1),
        ],
        axis=0)
    early_z = jnp.concatenate([line_up(att_za, 0, SPAN), line_up(att_za, PAIR, SAMP)], axis=0)
    project(0, early_x, early_z)
    for d in (1, 2, 3):
        ax_copy(d, 1).wait()
        az_copy(d, 1).wait()
    late_x = jnp.concatenate([att_xb[h * SPAN:(h + 1) * SPAN, :] for h in range(GROUP)], axis=1)
    late_z = line_up(att_zb, 0, SPAN)
    project(1, late_x, late_z)
    sums_z = [jnp.dot(one, wout_x[z], preferred_element_type=F32) for one in (early_x, late_x)]
    sums_x = [jnp.dot(one, wout_z[x], preferred_element_type=F32) for one in (early_z, late_z)]
    for part in range(2):
        sum_x, sum_z = sums_x[part], sums_z[part]
        in_x, in_z = ((sum_in_xa, sum_in_za), (sum_in_xb, sum_in_zb))[part]
        for d in (1, 2, 3):
            sum_z_copy(d, part).wait()
            sum_z = sum_z + in_z[d].astype(F32)
            sum_x_copy(d, part).wait()
            sum_x = sum_x + in_x[d].astype(F32)
        for total, cols in ((sum_z, slice(0, HALF)), (sum_x, slice(HALF, OUT))):
            if part == 0:
                out_ref[:SPAN, cols] = total[:SPAN].astype(BF16)
                out_ref[2 * SPAN:, cols] = total[SPAN:].astype(BF16)
            else:
                out_ref[SPAN:2 * SPAN, cols] = total.astype(BF16)

    for d in (1, 2, 3):
        slot_copy(d).wait_send()
    for d in (2, 3):
        page_copy(d).wait_send()
    for half in range(2):
        half_copy(half).wait_send()

    @pl.loop(0, 4)
    def _(k):
        @pl.loop(1, SOURCES)
        def _(i):
            @pl.when(k != 1)
            def _():
                y_copy(k, i).wait_send()

            @pl.when(k == 1)
            def _():
                half_y_copy(0, i).wait_send()
                half_y_copy(1, i).wait_send()


def local(hidden_in, norm_gain, w_query, w_keyval, w_out, kv_store, page_slots, page_counts):
    vmem = pl.BlockSpec(memory_space=pltpu.VMEM)
    anywhere = pl.BlockSpec(memory_space=pl.ANY)
    dma = pltpu.SemaphoreType.DMA
    slots = page_slots.transpose(2, 1, 0)
    return pl.pallas_call(
        layer_kernel,
        out_shape=pltpu.VMEM((ROWS, OUT), BF16),
        in_specs=[anywhere, anywhere, anywhere, anywhere, anywhere, anywhere, anywhere, anywhere],
        out_specs=vmem,
        scratch_shapes=[
            pltpu.SMEM((1, 128), jnp.int32),
            pltpu.VMEM((1, D), F32),
            pltpu.VMEM((CAP, 1, 8), jnp.int32),
            pltpu.VMEM((ROWS, D), BF16),
            pltpu.VMEM((D, 256), BF16),
            pltpu.VMEM((64, D), BF16),
            pltpu.VMEM((4, 1024, HALF), BF16),
            pltpu.VMEM((4, 1024, HALF), BF16),
            pltpu.VMEM((16, 2 * PAGE, HD), BF16),
            pltpu.VMEM((16, PAGE, HD), BF16),
            pltpu.VMEM((16, PAGE, HD), BF16),
            pltpu.VMEM((16, 2 * PAGE, HD), BF16),
            pltpu.VMEM((16, 2 * PAGE, HD), BF16),
            pltpu.VMEM((8, 128), jnp.int32),
            pltpu.VMEM((4, 8, 128), jnp.int32),
            pltpu.SMEM((4, 8, 128), jnp.int32),
            pltpu.VMEM((4, SOURCES, CAP, 2 * PAGE, HD), BF16),
            pltpu.VMEM((4, SOURCES, CAP, 2 * PAGE, HD), BF16),
            pltpu.VMEM((ROWS, 128), F32),
            pltpu.VMEM((ROWS, 256), F32),
            pltpu.VMEM((ROWS, 64), F32),
            pltpu.VMEM((2 * ROWS, HD), BF16),
            pltpu.VMEM((QPAD, HD), BF16),
            pltpu.VMEM((ROWS, HD), BF16),
            pltpu.VMEM((4, ROWS, HD), BF16),
            pltpu.VMEM((2, 4, ROWS, HD), BF16),
            pltpu.VMEM((HD, QPAD), F32),
            pltpu.VMEM((1, QPAD), F32),
            pltpu.VMEM((1, QPAD), F32),
            pltpu.VMEM((HD + 16, EARLY_CHUNK * CAP * PAGE), BF16),
            pltpu.VMEM((HD, 2 * PAIR + 128), F32),
            pltpu.VMEM((1, 2 * PAIR + 128), F32),
            pltpu.VMEM((1, 2 * PAIR + 128), F32),
            pltpu.VMEM((4, HD, PAIR + 128), BF16),
            pltpu.VMEM((4, HD, PAIR + 128), BF16),
            pltpu.VMEM((4, 2, PAIR + 128), F32),
            pltpu.VMEM((4, 2, PAIR + 128), F32),
            pltpu.VMEM((4, HD, PAIR), BF16),
            pltpu.VMEM((4, HD, PAIR), BF16),
            pltpu.VMEM((4, 2, PAIR), F32),
            pltpu.VMEM((4, 2, PAIR), F32),
            pltpu.VMEM((PAIR + 2 * SAMP, HD), BF16),
            pltpu.VMEM((PAIR, HD), BF16),
            pltpu.VMEM((GROUP * SAMP, HD), BF16),
            pltpu.VMEM((4 * PAIR, HD), BF16),
            pltpu.VMEM((4 * PAIR, HD), BF16),
            pltpu.VMEM((4, PAIR + 2 * SAMP, HD), BF16),
            pltpu.VMEM((4, PAIR, HD), BF16),
            pltpu.VMEM((4, EARLY, HALF), BF16),
            pltpu.VMEM((4, EARLY, HALF), BF16),
            pltpu.VMEM((4, SPAN, HALF), BF16),
            pltpu.VMEM((4, SPAN, HALF), BF16),
            pltpu.VMEM((4, EARLY, HALF), BF16),
            pltpu.VMEM((4, EARLY, HALF), BF16),
            pltpu.VMEM((4, SPAN, HALF), BF16),
            pltpu.VMEM((4, SPAN, HALF), BF16),
            dma((7,)), dma((4,)), dma((4,)),
            dma((4,)), dma((4,)), dma((4,)), dma((4,)), dma((4,)), dma((4,)),
            dma((5 * SOURCES,)), dma((5 * SOURCES,)),
            dma((12,)), dma((12,)), dma((8,)), dma((8,)), dma((8,)), dma((8,)),
            dma((8,)), dma((8,)),
            dma((8,)), dma((8,)), dma((8,)), dma((8,)), dma((8,)), dma((8,)),
            dma((8,)), dma((8,)), dma((8,)), dma((8,)), dma((8,)), dma((8,)),
        ],
        compiler_params=pltpu.CompilerParams(
            collective_id=1, has_side_effects=True, vmem_limit_bytes=62 * 2**20),
        cost_estimate=pl.CostEstimate(flops=17 * 10**9, bytes_accessed=19 * 10**6, transcendentals=27 * 10**6),
        name="layer",
    )(
        slots, page_counts, norm_gain.reshape(1, D), hidden_in, w_query, w_keyval.T, w_out,
        kv_store.reshape(16, 4, 2 * PAGE, HD))


def solution(mesh):
    return jax.shard_map(
        local,
        mesh=mesh,
        in_specs=(
            P("pool", None),
            P(),
            P(None, "tp"),
            P(None, "tp"),
            P("tp", None),
            P(("pool", "tp"), None, None, None, None),
            P(None, ("pool", "tp"), None),
            P("pool", None),
        ),
        out_specs=P("pool", "tp"),
        check_vma=False,
    )
```

```python
import math

import jax
import jax.numpy as jnp
from jax import lax
from jax.experimental import pallas as pl
from jax.experimental.pallas import tpu as pltpu
from jax.sharding import PartitionSpec as P

SAMP = 16
MESH = pl.DeviceIdType.MESH
F32 = jnp.float32
BF16 = jnp.bfloat16
PAGE = 128
HD = 128
CAP = 3
D = 8192
LOG2E = 1.4426950408889634
DEAD = 1e30
ROWS = 272
GROUP = 8
SPAN = 128
PAIR = 2 * SPAN
EARLY = 144
QROWS = GROUP * ROWS
QPAD = 2304
TILE = 256
FIRST_TILES = (0, 1, 2, 3, 8)
LATER_TILES = (4, 5, 6, 7)
SOURCES = 8
EARLY_CHUNK = 4
LAST_CHUNK = 2
EARLY_STEPS = 7
LAST_STEPS = 2
HALF = 256
PART = 512
OUT = 512
NT = (((1,), (1,)), ((), ()))
NN = (((1,), (0,)), ((), ()))
FAR_FIRST = (2, 1, 3)


def plane_offset(i):
    dy = jnp.where(i < 2, 0, jnp.where(i < 6, 1 + 2 * (i % 2), 2))
    dc = jnp.where((i >= 2) & (i < 6), (i - 2) // 2, i % 2)
    return dy, dc


def stage_offset(k):
    return jnp.where(k < 2, k, 5 - k)


def layer_kernel(
    slots_hbm, counts_hbm, gain_hbm, hidden_hbm, wq_hbm, wkv_hbm, wout_hbm, kv_hbm, out_ref,
    counts_ref, gain_ref, slots_own, hidden, wq, wkv, wout_x, wout_z, held0, keys1, values1, held2, held3, slots_out, slots_in, slots_smem,
    ysend, yrecv, squares, q_acc, kv_acc, qown, qall, piece, pieces, turn,
    acc, stat_m, stat_l, vt, turn_o, turn_m, turn_l,
    part_out_a, part_in_a, stat_out_a, stat_in_a, part_out_b, part_in_b, stat_out_b, stat_in_b,
    att_out_a, att_out_b, samples, att_xa, att_xb, att_za, att_zb,
    sum_out_xa, sum_in_xa, sum_out_xb, sum_in_xb, sum_out_za, sum_in_za, sum_out_zb, sum_in_zb,
    load_sem, wout_load_sem, slot_sem, zk_s, zk_r, zs_s, zs_r, zp_s, zp_r, y_s, y_r,
    xq_s, xq_r, xt_s, xt_r, xw_s, xw_r, zw_s, zw_r,
    xo_s, xo_r, xl_s, xl_r, xa_s, xa_r, za_s, za_r, xo2_s, xo2_r, zo_s, zo_r,
):
    pool = lax.axis_index("pool")
    tp = lax.axis_index("tp")
    y, c = pool // 2, pool % 2
    z, x = tp // 4, tp % 4
    scale = LOG2E / math.sqrt(HD)
    held = (held0, None, held2, held3)

    def x_peer(d):
        return (pool, z * 4 + (x + d) % 4)

    def z_peer(d):
        return (pool, ((z + d) % 4) * 4 + x)

    def plane_peer(i):
        dy, dc = plane_offset(i)
        return ((y + dy) % 4) * 2 + (c + dc) % 2

    def remote(src, dst, send_sem, recv_sem, device):
        return pltpu.make_async_remote_copy(
            src_ref=src, dst_ref=dst, send_sem=send_sem, recv_sem=recv_sem, device_id=device, device_id_type=MESH)

    own_pages = pltpu.make_async_copy(kv_hbm.at[:, z], held0, load_sem.at[0])
    own_pages.start()
    fetch_slots = pltpu.make_async_copy(slots_hbm, slots_own, load_sem.at[4])
    fetch_slots.start()
    loads = [
        pltpu.make_async_copy(hidden_hbm, hidden, load_sem.at[1]),
        pltpu.make_async_copy(wq_hbm, wq, load_sem.at[2]),
        pltpu.make_async_copy(wkv_hbm, wkv, load_sem.at[3]),
        pltpu.make_async_copy(gain_hbm, gain_ref, load_sem.at[5]),
        pltpu.make_async_copy(counts_hbm, counts_ref, load_sem.at[6]),
    ]
    barrier = pltpu.get_barrier_semaphore()
    for i in range(1, SOURCES):
        pl.semaphore_signal(barrier, inc=1, device_id=(plane_peer(i), tp), device_id_type=MESH)
    for d in (1, 2, 3):
        pl.semaphore_signal(barrier, inc=1, device_id=x_peer(d), device_id_type=MESH)
        pl.semaphore_signal(barrier, inc=1, device_id=z_peer(d), device_id_type=MESH)

    for load in loads:
        load.start()
    fetch_slots.wait()
    for slot in range(CAP):
        slots_out[slot:slot + 1, :8] = slots_own[slot]
    own_slots = pltpu.make_async_copy(slots_out, slots_smem.at[0], slot_sem.at[0])
    own_slots.start()
    pl.semaphore_wait(barrier, SOURCES - 1 + 6)

    def slot_copy(d):
        return remote(slots_out, slots_in.at[d], zs_s.at[d], zs_r.at[d], z_peer(d))

    def page_copy(d):
        return remote(kv_hbm.at[:, (z + d) % 4], held[d], zk_s.at[d], zk_r.at[d], z_peer(d))

    def half_copy(half):
        into = (keys1, values1)[half]
        source = kv_hbm.at[:, (z + 1) % 4, pl.ds(half * PAGE, PAGE)]
        return remote(source, into, zk_s.at[half], zk_r.at[half], z_peer(1))

    for d in (1, 3, 2):
        slot_copy(d).start()
    half_copy(0).start()
    page_copy(3).start()

    def y_copy(k, i):
        return remote(
            ysend.at[k, i], yrecv.at[k, i], y_s.at[k * SOURCES + i], y_r.at[k * SOURCES + i], (plane_peer(i), tp))

    def half_y_copy(half, i):
        rows = pl.ds(half * PAGE, PAGE)
        own = (1 + 3 * half) * SOURCES + i
        return remote(
            ysend.at[1, i, :, rows], yrecv.at[1, i, :, rows], y_s.at[own], y_r.at[own], (plane_peer(i), tp))

    def pass_on(k, d):
        for slot in range(CAP):
            yrecv[k, 0, slot] = held[d][slots_smem[d, slot, pool]]

        @pl.loop(1, SOURCES)
        def _(i):
            dest = plane_peer(i)
            for slot in range(CAP):
                ysend[k, i, slot] = held[d][slots_smem[d, slot, dest]]
            y_copy(k, i).start()

    def pass_half(half):
        pages = (keys1, values1)[half]
        rows = pl.ds(half * PAGE, PAGE)
        for slot in range(CAP):
            yrecv[1, 0, slot, rows] = pages[slots_smem[1, slot, pool]]

        @pl.loop(1, SOURCES)
        def _(i):
            dest = plane_peer(i)
            for slot in range(CAP):
                ysend[1, i, slot, rows] = pages[slots_smem[1, slot, dest]]
            half_y_copy(half, i).start()

    own_slots.wait()
    own_pages.wait()
    pass_on(0, 0)

    for load in loads:
        load.wait()
    squares[...] = jnp.zeros_like(squares)

    @pl.loop(0, D // PART)
    def _(n):
        part = hidden[:, pl.ds(pl.multiple_of(n * PART, PART), PART)].astype(F32)
        part = part * part
        squares[...] += (part[:, :128] + part[:, 128:256]) + (part[:, 256:384] + part[:, 384:])

    half_copy(1).start()
    mean = jnp.sum(squares[...], axis=1, keepdims=True) * (1.0 / D)
    squares[...] = jnp.broadcast_to(lax.rsqrt(mean + 1e-05), squares.shape)
    q_acc[...] = jnp.zeros_like(q_acc)
    kv_acc[...] = jnp.zeros_like(kv_acc)

    @pl.loop(0, D // PART)
    def _(n):
        cols = pl.ds(pl.multiple_of(n * PART, PART), PART)
        inverse = squares[:, :1]
        normed = (hidden[:, cols].astype(F32) * inverse * gain_ref[:, cols]).astype(BF16)
        q_acc[...] += jnp.dot(normed, wq[cols, :], preferred_element_type=F32)
        kv_acc[...] += lax.dot_general(normed, wkv[:, cols], NT, preferred_element_type=F32)

    queries = q_acc[...].astype(BF16)
    for h in range(2):
        head = queries[:, h * HD:(h + 1) * HD]
        qown[h * SPAN:(h + 1) * SPAN, :] = head[:SPAN]
        qown[PAIR + h * SPAN:PAIR + (h + 1) * SPAN, :] = head[SPAN:2 * SPAN]
        qown[2 * PAIR + h * SAMP:2 * PAIR + (h + 1) * SAMP, :] = head[2 * SPAN:]

    rows_a = pl.ds(pl.multiple_of(x * PAIR, PAIR), PAIR)
    rows_b = pl.ds(pl.multiple_of(GROUP * SPAN + x * PAIR, PAIR), PAIR)
    rows_c = pl.ds(2 * GROUP * SPAN, GROUP * SAMP)
    own_rows = (rows_a, rows_b, pl.ds(pl.multiple_of(2 * GROUP * SPAN + x * 2 * SAMP, 2 * SAMP), 2 * SAMP))
    made_rows = (pl.ds(0, PAIR), pl.ds(PAIR, PAIR), pl.ds(2 * PAIR, 2 * SAMP))

    def q_copy(d, n):
        return remote(
            qown.at[made_rows[n]], qall.at[own_rows[n]], xq_s.at[d * 3 + n], xq_r.at[d * 3 + n], x_peer(d))

    for n in range(3):
        for d in FAR_FIRST:
            q_copy(d, n).start()
        qall[own_rows[n], :] = qown[made_rows[n], :]
    qall[QROWS:, :] = jnp.zeros((QPAD - QROWS, HD), BF16)

    half = kv_acc[...]
    blank = jnp.zeros_like(half)
    piece[...] = jnp.where(
        x % 2 == 0, jnp.concatenate([half, blank], axis=1), jnp.concatenate([blank, half], axis=1)).astype(BF16)

    def piece_copy(d):
        return remote(piece, pieces.at[z], zp_s.at[d], zp_r.at[d], z_peer(d))

    for d in (1, 2, 3):
        piece_copy(d).start()
    pieces[z] = piece[...]

    def wout_columns(to_z, to_x, half):
        return pl.ds(pl.multiple_of((to_z * 4 + to_x) * OUT + half * HALF, HALF), HALF)

    def line_rows(place):
        return pl.ds(pl.multiple_of(place * 256, 256), 256)

    def wout_x_copy(d, n):
        part = 2 * c + n
        return remote(
            wout_hbm.at[:, wout_columns(part, (x + d) % 4, 0)], wout_x.at[part, line_rows(x)],
            xw_s.at[d * 2 + n], xw_r.at[d * 2 + n], x_peer(d))

    def wout_z_copy(d, n):
        part = 2 * c + n
        return remote(
            wout_hbm.at[:, wout_columns((z + d) % 4, part, 1)], wout_z.at[part, line_rows(z)],
            zw_s.at[d * 2 + n], zw_r.at[d * 2 + n], z_peer(d))

    def own_wout_x(n):
        part = 2 * c + n
        return pltpu.make_async_copy(
            wout_hbm.at[:, wout_columns(part, x, 0)], wout_x.at[part, line_rows(x)], wout_load_sem.at[n])

    def own_wout_z(n):
        part = 2 * c + n
        return pltpu.make_async_copy(
            wout_hbm.at[:, wout_columns(z, part, 1)], wout_z.at[part, line_rows(z)], wout_load_sem.at[2 + n])

    def wout_x_share(n):
        part = 2 * c + n
        return remote(wout_x.at[part], wout_x.at[part], xw_s.at[n], xw_r.at[n], (y * 2 + 1 - c, tp))

    def wout_z_share(n):
        part = 2 * c + n
        return remote(wout_z.at[part], wout_z.at[part], zw_s.at[n], zw_r.at[n], (y * 2 + 1 - c, tp))

    acc[...] = jnp.zeros_like(acc)
    vt[HD:, :] = jnp.ones_like(vt[HD:, :])
    stat_m[...] = jnp.full_like(stat_m, -DEAD)
    stat_l[...] = jnp.zeros_like(stat_l)

    def turn_copy(d, kind):
        return remote(
            pieces.at[kind * 2 + z // 2], turn.at[kind, x], xt_s.at[d * 2 + kind], xt_r.at[d * 2 + kind], x_peer(d))

    def numbers_arrived(d):
        slot_copy(d).wait_recv()
        to_smem = pltpu.make_async_copy(slots_in.at[d], slots_smem.at[d], slot_sem.at[d])
        to_smem.start()
        to_smem.wait()

    def arrived(d, k):
        page_copy(d).wait_recv()
        numbers_arrived(d)
        pass_on(k, d)

    for d in (1, 2, 3):
        for n in range(3):
            q_copy(d, n).wait()

    def o_copy(d, part):
        out, into = ((part_out_a, part_in_a), (part_out_b, part_in_b))[part]
        return remote(out.at[d], into.at[d], xo_s.at[d * 2 + part], xo_r.at[d * 2 + part], x_peer(d))

    def l_copy(d, part):
        out, into = ((stat_out_a, stat_in_a), (stat_out_b, stat_in_b))[part]
        return remote(out.at[d], into.at[d], xl_s.at[d * 2 + part], xl_r.at[d * 2 + part], x_peer(d))

    def send_part(part):
        for d in FAR_FIRST:
            start = ((x + d) % 4) * PAIR
            if part == 0:
                cols = pl.ds(pl.multiple_of(start, PAIR), PAIR)
                part_out_a[d, :, :PAIR] = acc[:, cols].astype(BF16)
                part_out_a[d, :, PAIR:] = acc[:, rows_c].astype(BF16)
                stat_out_a[d, 0:1, :PAIR] = stat_m[:, cols]
                stat_out_a[d, 0:1, PAIR:] = stat_m[:, rows_c]
                stat_out_a[d, 1:2, :PAIR] = stat_l[:, cols]
                stat_out_a[d, 1:2, PAIR:] = stat_l[:, rows_c]
            else:
                cols = pl.ds(pl.multiple_of(GROUP * SPAN + start, PAIR), PAIR)
                part_out_b[d] = acc[:, cols].astype(BF16)
                stat_out_b[d, 0:1, :] = stat_m[:, cols]
                stat_out_b[d, 1:2, :] = stat_l[:, cols]
            l_copy(d, part).start()
            o_copy(d, part).start()

    def own_turn():
        for d in (1, 2, 3):
            for kind in range(2):
                turn_copy(d, kind).wait()
        pair = (z % 2) * 2
        turn_keys = turn[0, pair] + turn[0, pair + 1]
        turn_values = turn[1, pair] + turn[1, pair + 1]
        rows = jnp.concatenate([qall[rows_a, :], qall[rows_c, :], qall[rows_b, :]], axis=0)
        count = 2 * PAIR + GROUP * SAMP
        scores = lax.dot_general(turn_keys, rows, NT, preferred_element_type=F32)
        key_idx = lax.broadcasted_iota(jnp.int32, (ROWS, count), 0)
        place = lax.broadcasted_iota(jnp.int32, (ROWS, count), 1)
        token = jnp.where(
            place < PAIR, place % SPAN,
            jnp.where(place < PAIR + GROUP * SAMP, 2 * SPAN + place % SAMP, SPAN + place % SPAN))
        allowed = (key_idx <= token) & ((key_idx < ROWS - SAMP) | (key_idx == token))
        scores = jnp.where(allowed, scores, -DEAD)
        top = jnp.max(scores, axis=0, keepdims=True)
        probs = jnp.exp2(scores * scale - top * scale)
        turn_m[...] = top
        turn_l[...] = jnp.sum(probs, axis=0, keepdims=True)
        turn_o[...] = lax.dot_general(turn_values.T, probs.astype(BF16), NN, preferred_element_type=F32)

    def attend(k, first, chunk, between=None):
        slots = chunk * CAP

        @pl.loop(0, chunk)
        def _(j):
            @pl.when((first + j > 0) & (k != 1))
            def _():
                y_copy(k, first + j).wait_recv()

            @pl.when((first + j > 0) & (k == 1))
            def _():
                half_y_copy(0, first + j).wait_recv()
                half_y_copy(1, first + j).wait_recv()

        live = []
        for j in range(chunk):
            dy, dc = plane_offset(first + j)
            holder = (((y + 4 - dy) % 4) * 2 + (c + dc) % 2) * 16 + ((z + 4 - stage_offset(k)) % 4) * 4 + x
            count = counts_ref[0, holder]
            for slot in range(CAP):
                live.append(count > slot)
        pages = yrecv[k, pl.ds(first, chunk)]
        keys = pages[:, :, :PAGE, :].reshape(slots * PAGE, HD)
        width = pl.ds(0, slots * PAGE)
        vt[:HD, width] = pages[:, :, PAGE:, :].reshape(slots * PAGE, HD).T

        def some(tiles):
            cols = [pl.ds(t * TILE, TILE) for t in tiles]
            all_scores = [lax.dot_general(keys, qall[own, :], NT, preferred_element_type=F32) for own in cols]
            for own, scores in zip(cols, all_scores):
                old_m = stat_m[:, own]
                new_m = old_m
                for j in range(slots):
                    top = jnp.max(scores[j * PAGE:(j + 1) * PAGE], axis=0, keepdims=True)
                    new_m = jnp.maximum(new_m, jnp.where(live[j], top, -DEAD))
                shift = new_m * scale
                shrink = jnp.exp2(old_m * scale - shift)
                weights = []
                for j in range(slots):
                    probs = jnp.exp2(scores[j * PAGE:(j + 1) * PAGE] * scale - jnp.where(live[j], shift, DEAD))
                    weights.append(probs.astype(BF16))
                blended = lax.dot_general(
                    vt[:, width], jnp.concatenate(weights, axis=0), NN, preferred_element_type=F32)
                acc[:, own] = acc[:, own] * shrink + blended[:HD]
                stat_m[:, own] = new_m
                stat_l[:, own] = stat_l[:, own] * shrink + blended[HD:HD + 1]

        some(FIRST_TILES)
        if between is not None:
            between()
        some(LATER_TILES)

    def early_step(n, carry):
        attend(n // 2, (n % 2) * EARLY_CHUNK, EARLY_CHUNK)

        @pl.when(n == 0)
        def _():
            numbers_arrived(1)
            half_copy(0).wait_recv()
            pass_half(0)

        @pl.when(n == 1)
        def _():
            half_copy(1).wait_recv()
            pass_half(1)
            arrived(3, 2)
            page_copy(2).start()
            for d in (1, 2, 3):
                piece_copy(d).wait()
            for d in FAR_FIRST:
                for kind in range(2):
                    turn_copy(d, kind).start()
            for kind in range(2):
                turn[kind, x] = pieces[kind * 2 + z // 2]
            for d in FAR_FIRST:
                for m in range(2):
                    wout_x_copy(d, m).start()
            for m in range(2):
                own_wout_x(m).start()
                own_wout_z(m).start()

        @pl.when(n == 2)
        def _():
            own_turn()

        @pl.when(n == 3)
        def _():
            arrived(2, 3)
            for d in FAR_FIRST:
                for m in range(2):
                    wout_z_copy(d, m).start()

        @pl.when(n == 5)
        def _():
            for m in range(2):
                for d in (1, 2, 3):
                    wout_x_copy(d, m).wait()
                own_wout_x(m).wait()
                wout_x_share(m).start()

        @pl.when(n == 6)
        def _():
            for m in range(2):
                for d in (1, 2, 3):
                    wout_z_copy(d, m).wait()
                own_wout_z(m).wait()
                wout_z_share(m).start()

        return carry

    def last_step(n, carry):
        def when_last(part):
            @pl.when(n == LAST_STEPS - 1)
            def _():
                send_part(part)

        attend(3, EARLY_CHUNK + n * LAST_CHUNK, LAST_CHUNK, lambda: when_last(0))
        when_last(1)

        return carry

    lax.fori_loop(0, EARLY_STEPS, early_step, 0)
    lax.fori_loop(0, LAST_STEPS, last_step, 0)

    def merge(own, part, turn_cols):
        into, stats = ((part_in_a, stat_in_a), (part_in_b, stat_in_b))[part]
        for d in (1, 2, 3):
            l_copy(d, part).wait()
            o_copy(d, part).wait()
        tops = [jnp.concatenate([stat_m[:, cols] for cols in own], axis=1) * scale, turn_m[:, turn_cols] * scale]
        sums = [jnp.concatenate([stat_l[:, cols] for cols in own], axis=1), turn_l[:, turn_cols]]
        sources = [jnp.concatenate([acc[:, cols] for cols in own], axis=1), turn_o[:, turn_cols]]
        for d in (1, 2, 3):
            tops.append(stats[d, 0:1, :] * scale)
            sums.append(stats[d, 1:2, :])
            sources.append(into[d].astype(F32))
        top = tops[0]
        for other in tops[1:]:
            top = jnp.maximum(top, other)
        shares = [jnp.exp2(one - top) for one in tops]
        norm = sums[0] * shares[0]
        for one, share in zip(sums[1:], shares[1:]):
            norm = norm + one * share
        inverse = 1.0 / norm
        merged = sources[0] * (shares[0] * inverse)
        for one, share in zip(sources[1:], shares[1:]):
            merged = merged + one * (share * inverse)
        return merged

    def ax_copy(d, part):
        out, into = ((att_out_a, att_xa), (att_out_b, att_xb))[part]
        return remote(
            out.at[pl.ds(0, PAIR)], into.at[rows_a], xa_s.at[d * 2 + part], xa_r.at[d * 2 + part], x_peer(d))

    def az_copy(d, part):
        out, into = ((att_out_a, att_za), (att_out_b, att_zb))[part]
        return remote(out, into.at[z], za_s.at[d * 2 + part], za_r.at[d * 2 + part], z_peer(d))

    merged = merge([rows_a, rows_c], 0, pl.ds(0, PAIR + GROUP * SAMP)).T.astype(BF16)
    samples[...] = merged[PAIR:]
    att_out_a[:PAIR, :] = merged[:PAIR]
    att_out_a[PAIR:, :] = samples[pl.ds(pl.multiple_of(x * 2 * SAMP, 2 * SAMP), 2 * SAMP), :]
    for d in FAR_FIRST:
        ax_copy(d, 0).start()
        az_copy(d, 0).start()
    att_xa[rows_a, :] = att_out_a[:PAIR, :]
    att_za[z] = att_out_a[...]
    att_out_b[...] = merge([rows_b], 1, pl.ds(PAIR + GROUP * SAMP, PAIR)).T.astype(BF16)
    for d in FAR_FIRST:
        ax_copy(d, 1).start()
        az_copy(d, 1).start()
    att_xb[rows_a, :] = att_out_b[...]
    att_zb[z] = att_out_b[...]

    def sum_z_copy(d, part):
        out, into = ((sum_out_za, sum_in_za), (sum_out_zb, sum_in_zb))[part]
        return remote(out.at[d], into.at[d], zo_s.at[d * 2 + part], zo_r.at[d * 2 + part], z_peer(d))

    def sum_x_copy(d, part):
        out, into = ((sum_out_xa, sum_in_xa), (sum_out_xb, sum_in_xb))[part]
        return remote(out.at[d], into.at[d], xo2_s.at[d * 2 + part], xo2_r.at[d * 2 + part], x_peer(d))

    def project(part, attended_x, attended_z):
        out_x, out_z = ((sum_out_xa, sum_out_za), (sum_out_xb, sum_out_zb))[part]
        for d in FAR_FIRST:
            out_x[d] = jnp.dot(attended_z, wout_z[(x + d) % 4], preferred_element_type=F32).astype(BF16)
            sum_x_copy(d, part).start()
            out_z[d] = jnp.dot(attended_x, wout_x[(z + d) % 4], preferred_element_type=F32).astype(BF16)
            sum_z_copy(d, part).start()

    def line_up(ref, start, size):
        return jnp.concatenate(
            [ref[m, start + h * size:start + (h + 1) * size, :] for m in range(4) for h in range(2)], axis=1)

    for m in range(2):
        wout_x_share(m).wait()
        wout_z_share(m).wait()
    for d in (1, 2, 3):
        ax_copy(d, 0).wait()
        az_copy(d, 0).wait()
    early_x = jnp.concatenate(
        [
            jnp.concatenate([att_xa[h * SPAN:(h + 1) * SPAN, :] for h in range(GROUP)], axis=1),
            jnp.concatenate([samples[h * SAMP:(h + 1) * SAMP, :] for h in range(GROUP)], axis=1),
        ],
        axis=0)
    early_z = jnp.concatenate([line_up(att_za, 0, SPAN), line_up(att_za, PAIR, SAMP)], axis=0)
    project(0, early_x, early_z)
    for d in (1, 2, 3):
        ax_copy(d, 1).wait()
        az_copy(d, 1).wait()
    late_x = jnp.concatenate([att_xb[h * SPAN:(h + 1) * SPAN, :] for h in range(GROUP)], axis=1)
    late_z = line_up(att_zb, 0, SPAN)
    project(1, late_x, late_z)
    sums_z = [jnp.dot(one, wout_x[z], preferred_element_type=F32) for one in (early_x, late_x)]
    sums_x = [jnp.dot(one, wout_z[x], preferred_element_type=F32) for one in (early_z, late_z)]
    for part in range(2):
        sum_x, sum_z = sums_x[part], sums_z[part]
        in_x, in_z = ((sum_in_xa, sum_in_za), (sum_in_xb, sum_in_zb))[part]
        for d in (1, 2, 3):
            sum_z_copy(d, part).wait()
            sum_z = sum_z + in_z[d].astype(F32)
            sum_x_copy(d, part).wait()
            sum_x = sum_x + in_x[d].astype(F32)
        for total, cols in ((sum_z, slice(0, HALF)), (sum_x, slice(HALF, OUT))):
            if part == 0:
                out_ref[:SPAN, cols] = total[:SPAN].astype(BF16)
                out_ref[2 * SPAN:, cols] = total[SPAN:].astype(BF16)
            else:
                out_ref[SPAN:2 * SPAN, cols] = total.astype(BF16)

    for d in (1, 2, 3):
        slot_copy(d).wait_send()
    for d in (2, 3):
        page_copy(d).wait_send()
    for half in range(2):
        half_copy(half).wait_send()

    @pl.loop(0, 4)
    def _(k):
        @pl.loop(1, SOURCES)
        def _(i):
            @pl.when(k != 1)
            def _():
                y_copy(k, i).wait_send()

            @pl.when(k == 1)
            def _():
                half_y_copy(0, i).wait_send()
                half_y_copy(1, i).wait_send()


def local(hidden_in, norm_gain, w_query, w_keyval, w_out, kv_store, page_slots, page_counts):
    vmem = pl.BlockSpec(memory_space=pltpu.VMEM)
    anywhere = pl.BlockSpec(memory_space=pl.ANY)
    dma = pltpu.SemaphoreType.DMA
    slots = page_slots.transpose(2, 1, 0)
    return pl.pallas_call(
        layer_kernel,
        out_shape=pltpu.VMEM((ROWS, OUT), BF16),
        in_specs=[anywhere, anywhere, anywhere, anywhere, anywhere, anywhere, anywhere, anywhere],
        out_specs=vmem,
        scratch_shapes=[
            pltpu.SMEM((1, 128), jnp.int32),
            pltpu.VMEM((1, D), F32),
            pltpu.VMEM((CAP, 1, 8), jnp.int32),
            pltpu.VMEM((ROWS, D), BF16),
            pltpu.VMEM((D, 256), BF16),
            pltpu.VMEM((64, D), BF16),
            pltpu.VMEM((4, 1024, HALF), BF16),
            pltpu.VMEM((4, 1024, HALF), BF16),
            pltpu.VMEM((16, 2 * PAGE, HD), BF16),
            pltpu.VMEM((16, PAGE, HD), BF16),
            pltpu.VMEM((16, PAGE, HD), BF16),
            pltpu.VMEM((16, 2 * PAGE, HD), BF16),
            pltpu.VMEM((16, 2 * PAGE, HD), BF16),
            pltpu.VMEM((8, 128), jnp.int32),
            pltpu.VMEM((4, 8, 128), jnp.int32),
            pltpu.SMEM((4, 8, 128), jnp.int32),
            pltpu.VMEM((4, SOURCES, CAP, 2 * PAGE, HD), BF16),
            pltpu.VMEM((4, SOURCES, CAP, 2 * PAGE, HD), BF16),
            pltpu.VMEM((ROWS, 128), F32),
            pltpu.VMEM((ROWS, 256), F32),
            pltpu.VMEM((ROWS, 64), F32),
            pltpu.VMEM((2 * ROWS, HD), BF16),
            pltpu.VMEM((QPAD, HD), BF16),
            pltpu.VMEM((ROWS, HD), BF16),
            pltpu.VMEM((4, ROWS, HD), BF16),
            pltpu.VMEM((2, 4, ROWS, HD), BF16),
            pltpu.VMEM((HD, QPAD), F32),
            pltpu.VMEM((1, QPAD), F32),
            pltpu.VMEM((1, QPAD), F32),
            pltpu.VMEM((HD + 16, EARLY_CHUNK * CAP * PAGE), BF16),
            pltpu.VMEM((HD, 2 * PAIR + 128), F32),
            pltpu.VMEM((1, 2 * PAIR + 128), F32),
            pltpu.VMEM((1, 2 * PAIR + 128), F32),
            pltpu.VMEM((4, HD, PAIR + 128), BF16),
            pltpu.VMEM((4, HD, PAIR + 128), BF16),
            pltpu.VMEM((4, 2, PAIR + 128), F32),
            pltpu.VMEM((4, 2, PAIR + 128), F32),
            pltpu.VMEM((4, HD, PAIR), BF16),
            pltpu.VMEM((4, HD, PAIR), BF16),
            pltpu.VMEM((4, 2, PAIR), F32),
            pltpu.VMEM((4, 2, PAIR), F32),
            pltpu.VMEM((PAIR + 2 * SAMP, HD), BF16),
            pltpu.VMEM((PAIR, HD), BF16),
            pltpu.VMEM((GROUP * SAMP, HD), BF16),
            pltpu.VMEM((4 * PAIR, HD), BF16),
            pltpu.VMEM((4 * PAIR, HD), BF16),
            pltpu.VMEM((4, PAIR + 2 * SAMP, HD), BF16),
            pltpu.VMEM((4, PAIR, HD), BF16),
            pltpu.VMEM((4, EARLY, HALF), BF16),
            pltpu.VMEM((4, EARLY, HALF), BF16),
            pltpu.VMEM((4, SPAN, HALF), BF16),
            pltpu.VMEM((4, SPAN, HALF), BF16),
            pltpu.VMEM((4, EARLY, HALF), BF16),
            pltpu.VMEM((4, EARLY, HALF), BF16),
            pltpu.VMEM((4, SPAN, HALF), BF16),
            pltpu.VMEM((4, SPAN, HALF), BF16),
            dma((7,)), dma((4,)), dma((4,)),
            dma((4,)), dma((4,)), dma((4,)), dma((4,)), dma((4,)), dma((4,)),
            dma((5 * SOURCES,)), dma((5 * SOURCES,)),
            dma((12,)), dma((12,)), dma((8,)), dma((8,)), dma((8,)), dma((8,)),
            dma((8,)), dma((8,)),
            dma((8,)), dma((8,)), dma((8,)), dma((8,)), dma((8,)), dma((8,)),
            dma((8,)), dma((8,)), dma((8,)), dma((8,)), dma((8,)), dma((8,)),
        ],
        compiler_params=pltpu.CompilerParams(
            collective_id=1, has_side_effects=True, vmem_limit_bytes=62 * 2**20),
        cost_estimate=pl.CostEstimate(flops=17 * 10**9, bytes_accessed=19 * 10**6, transcendentals=27 * 10**6),
        name="layer",
    )(
        slots, page_counts, norm_gain.reshape(1, D), hidden_in, w_query, w_keyval.T, w_out,
        kv_store.reshape(16, 4, 2 * PAGE, HD))


def solution(mesh):
    return jax.shard_map(
        local,
        mesh=mesh,
        in_specs=(
            P("pool", None),
            P(),
            P(None, "tp"),
            P(None, "tp"),
            P("tp", None),
            P(("pool", "tp"), None, None, None, None),
            P(None, ("pool", "tp"), None),
            P("pool", None),
        ),
        out_specs=P("pool", "tp"),
        check_vma=False,
    )
```
